512 devices in a mesh: seq: 64 (over z, y), ch: 8 (over x, core).
Axes of the slice: x: 4, y: 8, z: 8, core: 2. Of those that a mesh axis runs over, the one named last changes fastest.
Arguments:
- token_ids: int32 [32768], P('seq'), may hold values from 0 to 511
- embed_table: bfloat16 [512, 4096], P(None, 'ch')
- norm_gain: float32 [4096], P('ch'), may hold values from 0.5 to 1.5
- short_filters: float32 [2, 3, 7, 4096], P(None, None, None, 'ch')
- medium_filter: float32 [128, 4096], P(None, 'ch'), may hold values from -0.5 to 0.5
- mode_rates: float32 [16, 4096], P(None, 'ch'), as said below
- mode_residues: float32 [16, 4096], P(None, 'ch'), may hold values from -1.5 to 1.5
Outputs:
- result: bfloat16 [32768, 4096], P('seq', 'ch')
The draws below stay inside these ranges and needn't reach their ends.
Inputs may be any that keep to these rules, and one draw needn't show every extreme that they name: `mode_rates`: positive decay rates.
All inputs are finite; a program needn't handle non-finite values.
Results may differ from the reference program's by a relative error of at most 0.012.
The reference program's roundings to bfloat16 on the way count: a program that leaves them out, or rounds other values in their place, can miss the bound.
Values may be sent and summed in bfloat16 or wider, within the bound.
No kernel may reach another device: no remote copies, remote signals or barrier semaphores. Data moves between devices by JAX's collectives and lax.ppermute only.
A program may use at most 64 MiB of HBM per device.

```python
import jax
import jax.numpy as jnp
from jax import lax

C = 4096
VOCAB = 512
TAPS_S = 7
TAPS_M = 128
MODES = 16
TOKENS = 32768


def column_scales(key):
    key = jax.random.fold_in(key, 101)
    ramp = jnp.sqrt(1.0 + 2.0 * jnp.arange(C, dtype=jnp.float32) / (C - 1))
    return ramp * jnp.exp(jax.random.uniform(key, (C,), jnp.float32, -1.15, 1.15))


def draw_embed_table(key, part):
    column_scale = column_scales(key)[None, :]
    key = jax.random.fold_in(key, 7)
    first, second = jax.random.split(key, 2)
    base = jax.random.normal(first, (VOCAB, C), jnp.float32)
    row_scale = jnp.exp(jax.random.uniform(second, (VOCAB, 1), jnp.float32, -1.15, 1.15))
    return (0.5 * base * row_scale * column_scale).astype(jnp.bfloat16)


def draw_short_filters(key, part):
    column_scale = column_scales(key)
    key = jax.random.fold_in(key, 13)
    taps = jax.random.normal(key, (2, 3, TAPS_S, C), jnp.float32) / jnp.sqrt(jnp.float32(TAPS_S))
    factor = jnp.stack([2.0 / column_scale, jnp.ones_like(column_scale)], 0)[:, None, None, :]
    return (taps * factor).astype(jnp.float32)


def draw_mode_rates(key, part):
    key = jax.random.fold_in(key, 11)
    first, second, third = jax.random.split(key, 3)
    fast = jnp.exp(jax.random.uniform(first, (MODES, C), jnp.float32, jnp.log(1.0 / 50.0), jnp.log(1.0 / 30.0)))
    slow = jnp.exp(jax.random.uniform(second, (MODES, C), jnp.float32, jnp.log(0.1 / TOKENS), jnp.log(2.0 / TOKENS)))
    share = 0.5
    chosen = jax.random.uniform(third, (MODES, C), jnp.float32) < share
    return jnp.where(chosen, slow, fast).astype(jnp.float32)


def with_ends(values, own_key, low, high):
    longest = values.shape.index(max(values.shape))
    spots = []
    for shift in (0, 1):
        where = [jax.random.randint(jax.random.fold_in(own_key, axis), (), 0, length) for axis, length in enumerate(values.shape)]
        where[longest] = (where[longest] + shift) % values.shape[longest]
        spots.append(tuple(where))
    return values.at[spots[0]].set(low).at[spots[1]].set(high)


def block_levels(stream_key, extent, cuts, least, largest):
    factor_of, own = 1.0, jax.random.fold_in(stream_key, 6)
    for dim, shards_of in cuts:
        draws = jnp.exp(jax.random.uniform(jax.random.fold_in(own, dim), (shards_of,), jnp.float32, least / len(cuts), largest / len(cuts)))
        factor_of = factor_of * jnp.repeat(draws, extent[dim] // shards_of).reshape([-1 if axis == dim else 1 for axis in range(len(extent))])
    return factor_of


def bell_draw(rng, dims, scale, limit, shards=(), held_as=jnp.bfloat16):
    values = scale * jax.random.normal(rng, dims, jnp.float32)
    if shards:
        values = values * block_levels(rng, dims, shards, -0.22, 0.18)
    return jnp.clip(values, -limit, limit).astype(held_as)


def setup_inputs(seed: int = 0) -> dict:
    keys = jax.random.split(jax.random.key(seed), 8)
    return {
        "token_ids": with_ends(jax.random.randint(keys[0], (TOKENS,), 0, VOCAB), jax.random.fold_in(keys[0], 1), 0, VOCAB - 1).astype(jnp.int32),
        "embed_table": draw_embed_table(jax.random.fold_in(keys[7], 71), 0),
        "norm_gain": jnp.clip(1.0 + 0.1 * jax.random.normal(keys[2], (C,), jnp.float32), 0.5, 1.5),
        "short_filters": draw_short_filters(jax.random.fold_in(keys[7], 71), 0),
        "medium_filter": bell_draw(keys[4], (TAPS_M, C), TAPS_M ** -0.5, 0.5, ((1, 8),), jnp.float32),
        "mode_rates": draw_mode_rates(jax.random.fold_in(keys[7], 71), 0),
        "mode_residues": bell_draw(keys[6], (MODES, C), 0.25, 1.5, ((1, 8),), jnp.float32),
    }


def rounded(values):
    stored = values.astype(jnp.bfloat16)
    stored = lax.optimization_barrier(stored)
    return stored.astype(jnp.float32)

def causal_fir(signal, kernel):
    span = kernel.shape[0] - 1
    extended = jnp.pad(signal, ((span, 0), (0, 0)))
    return lax.conv_general_dilated(extended[None], jnp.flip(kernel, 0)[:, None, :], (1,), 'VALID', dimension_numbers=('NWC', 'WIO', 'NWC'), feature_group_count=kernel.shape[1], precision=lax.Precision.HIGHEST)[0]

def long_product(signal, kernel):
    length = signal.shape[0]
    total = 2 * length
    spectrum = jnp.fft.rfft(signal, total, axis=0) * jnp.fft.rfft(kernel, total, axis=0)
    return jnp.fft.irfft(spectrum, total, axis=0)[:length].astype(jnp.float32)

def reference(token_ids, embed_table, norm_gain, short_filters, medium_filter, mode_rates, mode_residues):
    squares = lax.optimization_barrier(jnp.sum(jnp.square(embed_table.astype(jnp.float32)), axis=1))
    inverse = lax.rsqrt(squares[token_ids] / C + 1e-06)
    group_width = 128
    group_count = C // group_width

    def split(array):
        return jnp.moveaxis(array.reshape(array.shape[:-1] + (group_count, group_width)), -2, 0)
    pieces = (split(embed_table), split(norm_gain), split(short_filters), split(medium_filter), split(mode_rates), split(mode_residues))

    def one_group(portion):
        table_part, gain_part, short_part, medium_part, rates_part, residue_part = portion
        embedded = table_part[token_ids].astype(jnp.float32)
        signal = rounded(embedded * inverse[:, None] * gain_part[None, :])
        query_one = causal_fir(signal, short_part[0, 0])
        gated = rounded(causal_fir(signal, short_part[0, 1]) * causal_fir(signal, short_part[0, 2]))
        middle = long_product(gated, medium_part)
        first_out = rounded(query_one * middle)
        query_two = causal_fir(first_out, short_part[1, 0])
        driven = rounded(causal_fir(first_out, short_part[1, 1]) * causal_fir(first_out, short_part[1, 2]))
        positions = jnp.arange(TOKENS, dtype=jnp.float32)
        coefficient = residue_part * jnp.sqrt(-jnp.expm1(-2.0 * rates_part))
        response = jnp.zeros((TOKENS, group_width), jnp.float32)
        for mode_index in range(MODES):
            response = response + coefficient[mode_index][None, :] * jnp.exp(-rates_part[mode_index][None, :] * positions[:, None])
        whole = long_product(driven, response)
        return (query_two * whole).astype(jnp.bfloat16)
    outputs = lax.map(one_group, pieces)
    return jnp.moveaxis(outputs, 0, 1).reshape(TOKENS, C)
```

```python
import functools

import jax
import jax.numpy as jnp
import ml_dtypes
import numpy as np
from jax import lax
from jax.experimental import pallas as pl
from jax.experimental.pallas import tpu as pltpu
from jax.sharding import PartitionSpec as P

F32 = jnp.float32
BF16 = jnp.bfloat16
LANES = 128
STEPS = 64
LINES = 8
HALO_STEPS = 18
SPAN = 6
EXT_STEPS = SPAN + HALO_STEPS + SPAN + STEPS
OUT_STEPS = EXT_STEPS - SPAN
HALO_IDS = 256
BLOCK = 16
SECOND_ROWS = (SPAN + STEPS) * LINES
FREQS = 672
INNER = 8
NT = (((1,), (1,)), ((), ()))


def step_times():
    lines = np.arange(LINES)
    halo = -HALO_STEPS * LINES + lines[None] * HALO_STEPS + np.arange(-SPAN, HALO_STEPS)[:, None]
    main = lines[None] * STEPS + np.arange(-SPAN, STEPS)[:, None]
    return np.concatenate([halo, main], 0)


def tables(taps):
    times = step_times()
    pair = np.arange(FREQS)
    freq = (pair // 16) * 8 + pair % 8 + 0.5
    quarter = np.where(pair % 16 < 8, 0.0, 0.25)
    origin = HALO_STEPS * LINES

    def wave(position):
        return np.cos(2 * np.pi * (np.outer(freq, position) / FREQS + quarter[:, None]))

    used = times[SPAN:].copy()
    valid = np.ones(used.shape, bool)
    valid[HALO_STEPS : HALO_STEPS + SPAN] = False
    valid &= used >= -(taps - 1 + SPAN)
    forward = wave((used + origin).reshape(-1)) * valid.reshape(1, -1)
    taps_wave = wave(np.arange(taps))
    halo_rows = times[SPAN + HALO_STEPS - SPAN : SPAN + HALO_STEPS].reshape(-1)
    main_rows = times[SPAN + HALO_STEPS + SPAN :].reshape(-1)
    back = wave(np.concatenate([halo_rows, main_rows]) + origin).T * (2.0 / FREQS)
    order = np.zeros((STEPS * LINES, STEPS * LINES), np.float32)
    order[main_rows, np.arange(main_rows.size)] = 1.0
    half = lambda a: np.asarray(a, np.float32).astype(ml_dtypes.bfloat16)
    return dict(
        forward=half(forward),
        taps_wave=split_wave(taps_wave),
        back=half(back),
        order=half(order),
    )


def split_wave(wave):
    high = np.asarray(wave, np.float32).astype(ml_dtypes.bfloat16)
    low = (wave - high.astype(np.float64)).astype(ml_dtypes.bfloat16)
    return np.concatenate([high, low, high], 1)


def lanes_of(group):
    return slice(group * LANES, (group + 1) * LANES)


def halves(values):
    high = values.astype(BF16)
    return high, (values - high.astype(F32)).astype(BF16)


def square_sums(table_ref, sums_ref):
    table = table_ref[...].astype(F32)
    high, low = halves(table * table)
    ones = jnp.ones((8, table.shape[1]), BF16)
    total = lax.dot_general(ones, high, NT, preferred_element_type=F32)
    total += lax.dot_general(ones, low, NT, preferred_element_type=F32)
    sums_ref[...] = jnp.broadcast_to(total[None, :1], sums_ref.shape)


def spectrum_of(wave_ref, medium_ref, spectrum_ref):
    high, low = halves(medium_ref[...])
    spectrum_ref[...] = jnp.dot(
        wave_ref[...], jnp.concatenate([high, high, low], 0), preferred_element_type=F32
    )


def one_hot(place, before, own, vocab):
    def digits(ids):
        high = lax.shift_right_arithmetic(ids, 4)
        low = ids - high * 16
        row = lax.broadcasted_iota(jnp.int32, (8, ids.shape[1]), 0)
        return jnp.where(row == 0, high, jnp.where(row == 1, low, 0)).astype(F32).astype(BF16)

    def picked(ids, first, steps, spread, shift):
        rows = steps * LINES
        row = lax.broadcasted_iota(jnp.int32, (rows, 1), 0)
        step = lax.shift_right_logical(row, 3)
        time = lax.bitwise_and(row, LINES - 1) * spread + step + shift
        column = lax.broadcasted_iota(jnp.int32, (rows, ids.shape[1]), 1) + first
        pick = jnp.where(column == time, 1.0, 0.0).astype(BF16)
        return lax.dot_general(pick, digits(ids), NT, preferred_element_type=F32)

    before = jnp.where(place > 0, before, -1)
    halo = picked(before, -HALO_IDS, SPAN + HALO_STEPS, HALO_STEPS, -LINES * HALO_STEPS - SPAN)
    edge = picked(before, -HALO_IDS, SPAN, STEPS, -SPAN)
    main = picked(own, 0, SPAN + STEPS, STEPS, -SPAN)
    column = jnp.concatenate([halo, edge + main[: SPAN * LINES], main[SPAN * LINES :]], 0)
    ids = (column[:, 0:1] * 16.0 + column[:, 1:2]).astype(jnp.int32)
    hot = ids == lax.broadcasted_iota(jnp.int32, (column.shape[0], vocab), 1)
    return jnp.where(hot, 1.0, 0.0).astype(BF16)


def taps_of(filters_ref, block, stream, group):
    return [
        jnp.broadcast_to(filters_ref[block, stream, d : d + 1, lanes_of(group)], (LINES, LANES))
        for d in range(SPAN + 1)
    ]


def tapped(window, taps, rows):
    total = None
    for d, tap in enumerate(taps):
        term = window[SPAN - d : SPAN - d + rows] * tap[None]
        total = term if total is None else total + term
    return total


def rows_at(start, size):
    return pl.ds(start if isinstance(start, int) else pl.multiple_of(start, 16), size)


def second_window(second_ref, b, group):
    rows = rows_at(b * BLOCK * LINES, (BLOCK + SPAN) * LINES)
    return second_ref[rows, lanes_of(group)].astype(F32).reshape(BLOCK + SPAN, LINES, LANES)


def driven_steps(driven_ref, b, group):
    rows = rows_at(b * BLOCK * LINES, BLOCK * LINES)
    return driven_ref[rows, lanes_of(group)].astype(F32).reshape(BLOCK, LINES, LANES)


def parts_of(kept_ref, modes):
    return (
        kept_ref.at[pl.ds(0, SECOND_ROWS)],
        kept_ref.at[pl.ds(SECOND_ROWS, STEPS * LINES)],
        kept_ref.at[pl.ds(SECOND_ROWS + STEPS * LINES, 2 * modes * LINES)],
    )


class Stage:
    def __init__(self, width, modes, kept_ref, ext_ref, gated_ref, query_ref, mixed_ref):
        self.width, self.modes = width, modes
        self.count = width // LANES
        self.second, self.driven, self.endings = parts_of(kept_ref, modes)
        self.ext, self.gated, self.query, self.mixed = ext_ref, gated_ref, query_ref, mixed_ref

    def embed(self, hot, scaled):
        rows = jnp.dot(hot, scaled, preferred_element_type=F32)
        self.ext[...] = rows.reshape(EXT_STEPS, LINES, self.width)

    def gate(self, filters_ref, at, steps):
        for g in range(self.count):
            window = self.ext[pl.ds(at, steps + SPAN), :, lanes_of(g)]
            key, value = [
                tapped(window, taps_of(filters_ref, 0, s, g), steps)
                for s in (1, 2)
            ]
            self.gated[rows_at(at * LINES, steps * LINES), lanes_of(g)] = (
                (key * value).reshape(steps * LINES, LANES).astype(BF16)
            )

    def ask(self, filters_ref, at, steps):
        for g in range(self.count):
            window = self.ext[pl.ds(at, steps + SPAN), :, lanes_of(g)]
            taps = taps_of(filters_ref, 0, 0, g)
            self.query[pl.ds(at, steps), :, lanes_of(g)] = tapped(window, taps, steps)

    def edges(self, filters_ref):
        gap = slice(HALO_STEPS * LINES, (HALO_STEPS + SPAN) * LINES)
        self.gated[gap, :] = jnp.zeros((SPAN * LINES, self.width), BF16)
        self.gate(filters_ref, 0, HALO_STEPS)
        self.ask(filters_ref, HALO_STEPS - SPAN, SPAN)

    def forward(self, forward_ref, spectrum_ref):
        wave = jnp.dot(forward_ref[...], self.gated[...], preferred_element_type=F32)
        wave = wave.reshape(FREQS // 16, 16, self.width)
        shape = spectrum_ref[...].reshape(FREQS // 16, 16, self.width)
        real, imag = wave[:, :8], wave[:, 8:]
        real_h, imag_h = shape[:, :8], shape[:, 8:]
        product = jnp.concatenate(
            [real * real_h - imag * imag_h, real * imag_h + imag * real_h], axis=1
        )
        self.mixed[...] = product.reshape(FREQS, self.width).astype(BF16)

    def backward(self, back_ref):
        middle = jnp.dot(back_ref[...], self.mixed[...], preferred_element_type=F32)
        middle = middle.reshape(SPAN + STEPS, LINES, self.width)
        halo = middle[:SPAN] * self.query[HALO_STEPS - SPAN : HALO_STEPS]
        halo = halo.astype(BF16).astype(F32)
        main = middle[SPAN:] * self.query[HALO_STEPS + SPAN :]
        main = main.reshape(STEPS * LINES, self.width).astype(BF16)
        self.second[SPAN * LINES :, :] = main
        last = main[(STEPS - SPAN) * LINES :].astype(F32).reshape(SPAN, LINES, self.width)
        first = []
        for k in range(SPAN):
            own = pltpu.roll(last[k], 1, 0)
            other = pltpu.roll(halo[k], 1, 0)
            line = lax.broadcasted_iota(jnp.int32, own.shape, 0)
            first.append(jnp.where(line == 0, other, own))
        self.second[: SPAN * LINES, :] = jnp.concatenate(first, 0).astype(BF16)

    def drive(self, filters_ref, b):
        for g in range(self.count):
            window = second_window(self.second, b, g)
            key, value = [
                tapped(window, taps_of(filters_ref, 1, s, g), BLOCK)
                for s in (1, 2)
            ]
            self.driven[rows_at(b * BLOCK * LINES, BLOCK * LINES), lanes_of(g)] = (
                (key * value).reshape(BLOCK * LINES, LANES).astype(BF16)
            )

    def decays(self, rates_ref, g):
        lanes = lanes_of(g)
        return [
            jnp.exp(-jnp.broadcast_to(rates_ref[r : r + 1, lanes], (LINES, LANES)))
            for r in range(self.modes)
        ]

    def absorb(self, decays, states, b, g):
        values = driven_steps(self.driven, b, g)
        for k in range(BLOCK):
            states = tuple(d * s + values[k] for d, s in zip(decays, states))
        return states

    def settle(self, rates_ref, state_ref, states, g):
        lanes = lanes_of(g)
        line = lax.broadcasted_iota(jnp.int32, (LINES, LANES), 0).astype(F32)
        for r in range(self.modes):
            self.endings[r * 2 * LINES : (r + 1) * 2 * LINES, lanes_of(g)] = jnp.concatenate(
                [h.astype(F32) for h in halves(states[r])], 0
            ).astype(BF16)
            weight = jnp.exp(-rates_ref[r : r + 1, lanes] * ((LINES - 1.0 - line) * STEPS))
            ending = jnp.sum(states[r] * weight, axis=0, keepdims=True).astype(state_ref.dtype)
            state_ref[0, r : r + 1, lanes] = ending


def first_part(
    channels,
    place_ref,
    squares_ref,
    before_ref,
    ids_ref,
    table_ref,
    gain_ref,
    filters_ref,
    rates_ref,
    forward_ref,
    spectrum_ref,
    back_ref,
    state_ref,
    kept_ref,
    ext_ref,
    gated_ref,
    query_ref,
    mixed_ref,
    forward_v,
    back_v,
    sems,
):
    loads = [
        pltpu.make_async_copy(forward_ref, forward_v, sems.at[0]),
        pltpu.make_async_copy(back_ref, back_v, sems.at[1]),
    ]
    for load in loads:
        load.start()
    vocab, width = table_ref.shape
    modes = rates_ref.shape[0]
    stage = Stage(width, modes, kept_ref, ext_ref, gated_ref, query_ref, mixed_ref)
    before = before_ref[:, before_ref.shape[1] - HALO_IDS :]
    hot = one_hot(place_ref[0], before, ids_ref[...], vocab)
    inverse = lax.rsqrt(jnp.sum(squares_ref[...], axis=0) / channels + 1e-06)
    column = jnp.transpose(jnp.broadcast_to(inverse, (8, vocab)))[:, 0:1]
    scaled = (table_ref[...].astype(F32) * column * gain_ref[...]).astype(BF16)
    main = HALO_STEPS + SPAN

    def loop(body):
        def step(i, carry):
            body(i)
            return carry

        lax.fori_loop(0, STEPS // BLOCK, step, 0)

    stage.embed(hot, scaled)
    stage.edges(filters_ref)

    def convolve(i):
        stage.gate(filters_ref, main + i * BLOCK, BLOCK)
        stage.ask(filters_ref, main + i * BLOCK, BLOCK)

    loop(convolve)
    loads[0].wait()
    stage.forward(forward_v, spectrum_ref)
    loads[1].wait()
    stage.backward(back_v)
    loop(lambda i: stage.drive(filters_ref, i))
    zero = jnp.zeros((LINES, LANES), F32)
    for g in range(stage.count):
        decays = stage.decays(rates_ref, g)

        def gather(i, states, g=g, decays=decays):
            return stage.absorb(decays, states, i, g)

        states = lax.fori_loop(0, STEPS // BLOCK, gather, (zero,) * modes)
        stage.settle(rates_ref, state_ref, states, g)
    for k in range(1, state_ref.shape[0]):
        state_ref[k] = state_ref[0]


def coefficients(rates, residues):
    double = 2.0 * rates
    series = double * (1.0 + double * (-0.5 + double * (1.0 / 6 + double * (-1.0 / 24))))
    return residues * jnp.sqrt(jnp.where(double < 0.02, series, 1.0 - jnp.exp(-double)))


def near_part(place_ref, rows_ref, rates_ref, near_ref, total_ref):
    across = jnp.exp(-rates_ref[...] * (1.0 * STEPS * LINES))
    own = lax.rem(place_ref[0], rows_ref.shape[0])
    total = jnp.zeros(rates_ref.shape, F32)
    near = total
    for j in range(rows_ref.shape[0]):
        near = jnp.where(own == j, total, near)
        total = across * total + rows_ref[j].astype(F32)
    near_ref[...] = near
    total_ref[...] = jnp.broadcast_to(total.astype(BF16)[None], total_ref.shape)


def second_part(
    filters_ref,
    rates_ref,
    residues_ref,
    kept_ref,
    order_ref,
    query_ref,
    whole_ref,
    weights_ref,
    query_v,
    whole_v,
    order_v,
    sems,
):
    load = pltpu.make_async_copy(order_ref, order_v, sems.at[0])
    load.start()
    weights_ref[...] = coefficients(rates_ref[...], residues_ref[...])
    modes, width = rates_ref.shape
    groups = width // LANES
    index = lax.broadcasted_iota(jnp.int32, (LINES, LANES), 0)
    second_ref, driven_ref, endings_ref = parts_of(kept_ref, modes)
    for group in range(groups):
        taps = taps_of(filters_ref, 1, 0, group)

        def conv_query(b, carry, group=group, taps=taps):
            window = second_window(second_ref, b, group)
            rows = pl.ds(pl.multiple_of(b * BLOCK * LINES, BLOCK * LINES), BLOCK * LINES)
            query_v[rows, lanes_of(group)] = (
                tapped(window, taps, BLOCK).reshape(BLOCK * LINES, LANES).astype(BF16)
            )
            return carry

        lax.fori_loop(0, STEPS // BLOCK, conv_query, 0)

        decays, weights, starts = [], [], []
        for r in range(modes):
            rate = jnp.broadcast_to(rates_ref[r : r + 1, lanes_of(group)], (LINES, LANES))
            ending = endings_ref[r * 2 * LINES : (r + 1) * 2 * LINES, lanes_of(group)].astype(F32)
            total = ending[:LINES] + ending[LINES:]
            for k in (1, 2, 4):
                moved = jnp.where(index >= k, pltpu.roll(total, k, 0), 0.0)
                total = total + jnp.exp(-rate * (1.0 * STEPS * k)) * moved
            starts.append(jnp.where(index >= 1, pltpu.roll(total, 1, 0), 0.0))
            decays.append(jnp.exp(-rate))
            weights.append(
                jnp.broadcast_to(weights_ref[r : r + 1, lanes_of(group)], (LINES, LANES))
            )

        def respond(b, states, group=group, decays=decays, weights=weights):
            values = driven_steps(driven_ref, b, group)
            outs = []
            for k in range(BLOCK):
                states = tuple(d * s + values[k] for d, s in zip(decays, states))
                sums = [w * s for w, s in zip(weights, states)]
                while len(sums) > 1:
                    sums = [a + b for a, b in zip(sums[0::2], sums[1::2])]
                outs.append(sums[0])
            rows = pl.ds(pl.multiple_of(b * BLOCK * LINES, BLOCK * LINES), BLOCK * LINES)
            whole_v[rows, lanes_of(group)] = jnp.concatenate(outs, 0)
            return states

        lax.fori_loop(0, STEPS // BLOCK, respond, tuple(starts))
    load.wait()
    query_ref[...] = jnp.dot(
        order_v[...], query_v[...], preferred_element_type=F32
    ).astype(BF16)
    high, low = halves(whole_v[...])
    whole_ref[...] = jnp.dot(order_v[...], high, preferred_element_type=F32) + jnp.dot(
        order_v[...], low, preferred_element_type=F32
    )


def third_part(
    inner,
    place_ref,
    near_ref,
    totals_ref,
    rates_ref,
    weights_ref,
    query_ref,
    whole_ref,
    out_ref,
    result_v,
    sems,
):
    modes, width = rates_ref.shape
    groups = width // LANES
    span = 1.0 * STEPS * LINES
    across = jnp.exp(-rates_ref[...] * (span * inner))
    own = lax.rem(place_ref[0], inner)
    rank = lax.div(place_ref[0], inner)
    far = jnp.zeros(rates_ref.shape, F32)
    for j in range(totals_ref.shape[0]):
        far = jnp.where(j < rank, across * far + totals_ref[j].astype(F32), far)
    incoming = near_ref[...] + jnp.exp(-rates_ref[...] * (span * own.astype(F32))) * far

    stores = []
    across = jnp.exp(-rates_ref[...] * LINES)
    entering = weights_ref[...] * incoming
    line = lax.broadcasted_iota(jnp.int32, (LINES, LANES), 0).astype(F32)
    for group in range(groups):
        decays, terms = [], []
        for r in range(modes):
            decays.append(jnp.broadcast_to(across[r : r + 1, lanes_of(group)], (LINES, LANES)))
            rise = jnp.exp(-rates_ref[r : r + 1, lanes_of(group)] * (line + 1.0))
            terms.append(rise * entering[r : r + 1, lanes_of(group)])

        def lift(b, terms, group=group, decays=decays):
            rows = pl.ds(pl.multiple_of(b * 64, 64), 64)
            outs = []
            for k in range(8):
                sums = list(terms)
                while len(sums) > 1:
                    sums = [a + b for a, b in zip(sums[0::2], sums[1::2])]
                outs.append(sums[0])
                terms = tuple(t * d for t, d in zip(terms, decays))
            whole = whole_ref[rows, lanes_of(group)] + jnp.concatenate(outs, 0)
            query = query_ref[rows, lanes_of(group)].astype(F32)
            result_v[rows, lanes_of(group)] = (query * whole).astype(BF16)
            return terms

        lax.fori_loop(0, STEPS // 8, lift, tuple(terms))
        stores.append(
            pltpu.make_async_copy(
                result_v.at[:, lanes_of(group)], out_ref.at[:, lanes_of(group)], sems.at[group]
            )
        )
        stores[-1].start()
    for store in stores:
        store.wait()


VMEM = pl.BlockSpec(memory_space=pltpu.VMEM)
SMEM = pl.BlockSpec(memory_space=pltpu.SMEM)
HBM = pl.BlockSpec(memory_space=pl.ANY)


FAR = pl.BlockSpec(memory_space=pltpu.HBM)


def far(array):
    return pltpu.with_memory_space_constraint(jnp.asarray(array), pltpu.HBM)


def cost(flops, moved):
    return pl.CostEstimate(flops=int(flops), bytes_accessed=int(moved), transcendentals=0)


def call(
    kernel, name, ins, outs, scratch=(), sems=0, out_space=None, limit=24, flops=1e9, moved=4e6
):
    return pl.pallas_call(
        kernel,
        name=name,
        in_specs=ins,
        out_specs=[out_space or VMEM] * len(outs),
        out_shape=[jax.ShapeDtypeStruct(*o) for o in outs],
        scratch_shapes=[pltpu.VMEM(*s) for s in scratch]
        + ([pltpu.SemaphoreType.DMA((sems,))] if sems else []),
        compiler_params=pltpu.CompilerParams(vmem_limit_bytes=limit << 20),
        cost_estimate=cost(flops, moved),
    )


def local(
    token_ids, embed_table, norm_gain, short_filters, medium_filter, mode_rates, mode_residues
):
    vocab, width = embed_table.shape
    count = token_ids.shape[0]
    modes = mode_rates.shape[0]
    taps = medium_filter.shape[0]
    shards = lax.axis_size("ch")
    length = lax.axis_size("seq")
    inner = min(INNER, length)
    near_groups = [[o * inner + i for i in range(inner)] for o in range(length // inner)]
    far_groups = [[o * inner + i for o in range(length // inner)] for i in range(inner)]
    const = tables(taps)
    place = jnp.reshape(lax.axis_index("seq").astype(jnp.int32), (1,))

    before = lax.ppermute(token_ids, "seq", [(i, i + 1) for i in range(length - 1)])
    (partial,) = call(
        square_sums, "square_sums", [VMEM], [((shards, 1, vocab), F32)], limit=8
    )(embed_table)
    squares = lax.all_to_all(partial, "ch", 0, 0)
    (spectrum,) = call(
        spectrum_of, "spectrum_of", [VMEM] * 2, [((FREQS, width), F32)], limit=8
    )(const["taps_wave"], medium_filter)
    kept_shape = (SECOND_ROWS + STEPS * LINES + 2 * modes * LINES, width)
    state, kept = call(
        functools.partial(first_part, channels_of(width, shards)),
        "first_part",
        [SMEM] + [VMEM] * 7 + [FAR, VMEM, FAR],
        [((inner, modes, width), BF16), (kept_shape, BF16)],
        [
            ((EXT_STEPS, LINES, width), F32),
            ((OUT_STEPS * LINES, width), BF16),
            ((OUT_STEPS, LINES, width), F32),
            ((FREQS, width), BF16),
            (const["forward"].shape, BF16),
            (const["back"].shape, BF16),
        ],
        sems=2,
    )(
        place,
        squares,
        before[None],
        token_ids[None],
        embed_table,
        norm_gain[None],
        short_filters,
        mode_rates,
        far(const["forward"]),
        spectrum,
        far(const["back"]),
    )
    rows = lax.all_to_all(state, "seq", 0, 0, axis_index_groups=near_groups, tiled=True)
    query, whole, weights = call(
        second_part,
        "second_part",
        [VMEM] * 4 + [FAR],
        [((count, width), BF16), ((count, width), F32), ((modes, width), F32)],
        [((count, width), BF16), ((count, width), F32), ((count, count), BF16)],
        sems=1,
        flops=4e9,
        moved=1e7,
    )(short_filters, mode_rates, mode_residues, kept, far(const["order"]))
    near, totals = call(
        near_part,
        "near_part",
        [SMEM] + [VMEM] * 2,
        [((modes, width), F32), ((length // inner, modes, width), BF16)],
        limit=4,
    )(place, rows, mode_rates)
    totals = lax.all_to_all(totals, "seq", 0, 0, axis_index_groups=far_groups, tiled=True)
    (out,) = call(
        functools.partial(third_part, inner),
        "third_part",
        [SMEM] + [VMEM] * 6,
        [((count, width), BF16)],
        [((count, width), BF16)],
        sems=width // LANES,
        out_space=HBM,
        limit=12,
    )(place, near, totals, mode_rates, weights, query, whole)
    return out


def channels_of(width, shards):
    return width * shards


def solution(mesh):
    placed = (
        P("seq"),
        P(None, "ch"),
        P("ch"),
        P(None, None, None, "ch"),
        P(None, "ch"),
        P(None, "ch"),
        P(None, "ch"),
    )
    return jax.shard_map(
        local, mesh=mesh, in_specs=placed, out_specs=P("seq", "ch"), check_vma=False
    )
```

```python
import functools

import jax
import jax.numpy as jnp
import ml_dtypes
import numpy as np
from jax import lax
from jax.experimental import pallas as pl
from jax.experimental.pallas import tpu as pltpu
from jax.sharding import PartitionSpec as P

F32 = jnp.float32
BF16 = jnp.bfloat16
LANES = 128
STEPS = 64
LINES = 8
HALO_STEPS = 18
SPAN = 6
EXT_STEPS = SPAN + HALO_STEPS + SPAN + STEPS
OUT_STEPS = EXT_STEPS - SPAN
HALO_IDS = 256
BLOCK = 16
SECOND_ROWS = (SPAN + STEPS) * LINES
FREQS = 672
INNER = 8
NT = (((1,), (1,)), ((), ()))


def step_times():
    lines = np.arange(LINES)
    halo = -HALO_STEPS * LINES + lines[None] * HALO_STEPS + np.arange(-SPAN, HALO_STEPS)[:, None]
    main = lines[None] * STEPS + np.arange(-SPAN, STEPS)[:, None]
    return np.concatenate([halo, main], 0)


def tables(taps):
    times = step_times()
    pair = np.arange(FREQS)
    freq = (pair // 16) * 8 + pair % 8 + 0.5
    quarter = np.where(pair % 16 < 8, 0.0, 0.25)
    origin = HALO_STEPS * LINES

    def wave(position):
        return np.cos(2 * np.pi * (np.outer(freq, position) / FREQS + quarter[:, None]))

    used = times[SPAN:].copy()
    valid = np.ones(used.shape, bool)
    valid[HALO_STEPS : HALO_STEPS + SPAN] = False
    valid &= used >= -(taps - 1 + SPAN)
    forward = wave((used + origin).reshape(-1)) * valid.reshape(1, -1)
    taps_wave = wave(np.arange(taps))
    halo_rows = times[SPAN + HALO_STEPS - SPAN : SPAN + HALO_STEPS].reshape(-1)
    main_rows = times[SPAN + HALO_STEPS + SPAN :].reshape(-1)
    back = wave(np.concatenate([halo_rows, main_rows]) + origin).T * (2.0 / FREQS)
    order = np.zeros((STEPS * LINES, STEPS * LINES), np.float32)
    order[main_rows, np.arange(main_rows.size)] = 1.0
    half = lambda a: np.asarray(a, np.float32).astype(ml_dtypes.bfloat16)
    return dict(
        forward=half(forward),
        taps_wave=split_wave(taps_wave),
        back=half(back),
        order=half(order),
    )


def split_wave(wave):
    high = np.asarray(wave, np.float32).astype(ml_dtypes.bfloat16)
    low = (wave - high.astype(np.float64)).astype(ml_dtypes.bfloat16)
    return np.concatenate([high, low, high], 1)


def lanes_of(group):
    return slice(group * LANES, (group + 1) * LANES)


def halves(values):
    high = values.astype(BF16)
    return high, (values - high.astype(F32)).astype(BF16)


def square_sums(table_ref, sums_ref):
    table = table_ref[...].astype(F32)
    high, low = halves(table * table)
    ones = jnp.ones((8, table.shape[1]), BF16)
    total = lax.dot_general(ones, high, NT, preferred_element_type=F32)
    total += lax.dot_general(ones, low, NT, preferred_element_type=F32)
    sums_ref[...] = jnp.broadcast_to(total[None, :1], sums_ref.shape)


def spectrum_of(wave_ref, medium_ref, spectrum_ref):
    high, low = halves(medium_ref[...])
    spectrum_ref[...] = jnp.dot(
        wave_ref[...], jnp.concatenate([high, high, low], 0), preferred_element_type=F32
    )


def one_hot(place, before, own, vocab):
    def digits(ids):
        high = lax.shift_right_arithmetic(ids, 4)
        low = ids - high * 16
        row = lax.broadcasted_iota(jnp.int32, (8, ids.shape[1]), 0)
        return jnp.where(row == 0, high, jnp.where(row == 1, low, 0)).astype(F32).astype(BF16)

    def picked(ids, first, steps, spread, shift):
        rows = steps * LINES
        row = lax.broadcasted_iota(jnp.int32, (rows, 1), 0)
        step = lax.shift_right_logical(row, 3)
        time = lax.bitwise_and(row, LINES - 1) * spread + step + shift
        column = lax.broadcasted_iota(jnp.int32, (rows, ids.shape[1]), 1) + first
        pick = jnp.where(column == time, 1.0, 0.0).astype(BF16)
        return lax.dot_general(pick, digits(ids), NT, preferred_element_type=F32)

    before = jnp.where(place > 0, before, -1)
    halo = picked(before, -HALO_IDS, SPAN + HALO_STEPS, HALO_STEPS, -LINES * HALO_STEPS - SPAN)
    edge = picked(before, -HALO_IDS, SPAN, STEPS, -SPAN)
    main = picked(own, 0, SPAN + STEPS, STEPS, -SPAN)
    column = jnp.concatenate([halo, edge + main[: SPAN * LINES], main[SPAN * LINES :]], 0)
    ids = (column[:, 0:1] * 16.0 + column[:, 1:2]).astype(jnp.int32)
    hot = ids == lax.broadcasted_iota(jnp.int32, (column.shape[0], vocab), 1)
    return jnp.where(hot, 1.0, 0.0).astype(BF16)


def taps_of(filters_ref, block, stream, group):
    return [
        jnp.broadcast_to(filters_ref[block, stream, d : d + 1, lanes_of(group)], (LINES, LANES))
        for d in range(SPAN + 1)
    ]


def tapped(window, taps, rows):
    total = None
    for d, tap in enumerate(taps):
        term = window[SPAN - d : SPAN - d + rows] * tap[None]
        total = term if total is None else total + term
    return total


def rows_at(start, size):
    return pl.ds(start if isinstance(start, int) else pl.multiple_of(start, 16), size)


def second_window(second_ref, b, group):
    rows = rows_at(b * BLOCK * LINES, (BLOCK + SPAN) * LINES)
    return second_ref[rows, lanes_of(group)].astype(F32).reshape(BLOCK + SPAN, LINES, LANES)


def driven_steps(driven_ref, b, group):
    rows = rows_at(b * BLOCK * LINES, BLOCK * LINES)
    return driven_ref[rows, lanes_of(group)].astype(F32).reshape(BLOCK, LINES, LANES)


def parts_of(kept_ref, modes):
    return (
        kept_ref.at[pl.ds(0, SECOND_ROWS)],
        kept_ref.at[pl.ds(SECOND_ROWS, STEPS * LINES)],
        kept_ref.at[pl.ds(SECOND_ROWS + STEPS * LINES, 2 * modes * LINES)],
    )


class Stage:
    def __init__(self, width, modes, kept_ref, ext_ref, gated_ref, query_ref, mixed_ref):
        self.width, self.modes = width, modes
        self.count = width // LANES
        self.second, self.driven, self.endings = parts_of(kept_ref, modes)
        self.ext, self.gated, self.query, self.mixed = ext_ref, gated_ref, query_ref, mixed_ref

    def embed(self, hot, scaled):
        rows = jnp.dot(hot, scaled, preferred_element_type=F32)
        self.ext[...] = rows.reshape(EXT_STEPS, LINES, self.width)

    def gate(self, filters_ref, at, steps):
        for g in range(self.count):
            window = self.ext[pl.ds(at, steps + SPAN), :, lanes_of(g)]
            key, value = [
                tapped(window, taps_of(filters_ref, 0, s, g), steps)
                for s in (1, 2)
            ]
            self.gated[rows_at(at * LINES, steps * LINES), lanes_of(g)] = (
                (key * value).reshape(steps * LINES, LANES).astype(BF16)
            )

    def ask(self, filters_ref, at, steps):
        for g in range(self.count):
            window = self.ext[pl.ds(at, steps + SPAN), :, lanes_of(g)]
            taps = taps_of(filters_ref, 0, 0, g)
            self.query[pl.ds(at, steps), :, lanes_of(g)] = tapped(window, taps, steps)

    def edges(self, filters_ref):
        gap = slice(HALO_STEPS * LINES, (HALO_STEPS + SPAN) * LINES)
        self.gated[gap, :] = jnp.zeros((SPAN * LINES, self.width), BF16)
        self.gate(filters_ref, 0, HALO_STEPS)
        self.ask(filters_ref, HALO_STEPS - SPAN, SPAN)

    def forward(self, forward_ref, spectrum_ref):
        wave = jnp.dot(forward_ref[...], self.gated[...], preferred_element_type=F32)
        wave = wave.reshape(FREQS // 16, 16, self.width)
        shape = spectrum_ref[...].reshape(FREQS // 16, 16, self.width)
        real, imag = wave[:, :8], wave[:, 8:]
        real_h, imag_h = shape[:, :8], shape[:, 8:]
        product = jnp.concatenate(
            [real * real_h - imag * imag_h, real * imag_h + imag * real_h], axis=1
        )
        self.mixed[...] = product.reshape(FREQS, self.width).astype(BF16)

    def backward(self, back_ref):
        middle = jnp.dot(back_ref[...], self.mixed[...], preferred_element_type=F32)
        middle = middle.reshape(SPAN + STEPS, LINES, self.width)
        halo = middle[:SPAN] * self.query[HALO_STEPS - SPAN : HALO_STEPS]
        halo = halo.astype(BF16).astype(F32)
        main = middle[SPAN:] * self.query[HALO_STEPS + SPAN :]
        main = main.reshape(STEPS * LINES, self.width).astype(BF16)
        self.second[SPAN * LINES :, :] = main
        last = main[(STEPS - SPAN) * LINES :].astype(F32).reshape(SPAN, LINES, self.width)
        first = []
        for k in range(SPAN):
            own = pltpu.roll(last[k], 1, 0)
            other = pltpu.roll(halo[k], 1, 0)
            line = lax.broadcasted_iota(jnp.int32, own.shape, 0)
            first.append(jnp.where(line == 0, other, own))
        self.second[: SPAN * LINES, :] = jnp.concatenate(first, 0).astype(BF16)

    def drive(self, filters_ref, b):
        for g in range(self.count):
            window = second_window(self.second, b, g)
            key, value = [
                tapped(window, taps_of(filters_ref, 1, s, g), BLOCK)
                for s in (1, 2)
            ]
            self.driven[rows_at(b * BLOCK * LINES, BLOCK * LINES), lanes_of(g)] = (
                (key * value).reshape(BLOCK * LINES, LANES).astype(BF16)
            )

    def decays(self, rates_ref, g):
        lanes = lanes_of(g)
        return [
            jnp.exp(-jnp.broadcast_to(rates_ref[r : r + 1, lanes], (LINES, LANES)))
            for r in range(self.modes)
        ]

    def absorb(self, decays, states, b, g):
        values = driven_steps(self.driven, b, g)
        for k in range(BLOCK):
            states = tuple(d * s + values[k] for d, s in zip(decays, states))
        return states

    def settle(self, rates_ref, state_ref, states, g):
        lanes = lanes_of(g)
        line = lax.broadcasted_iota(jnp.int32, (LINES, LANES), 0).astype(F32)
        for r in range(self.modes):
            self.endings[r * 2 * LINES : (r + 1) * 2 * LINES, lanes_of(g)] = jnp.concatenate(
                [h.astype(F32) for h in halves(states[r])], 0
            ).astype(BF16)
            weight = jnp.exp(-rates_ref[r : r + 1, lanes] * ((LINES - 1.0 - line) * STEPS))
            ending = jnp.sum(states[r] * weight, axis=0, keepdims=True).astype(state_ref.dtype)
            state_ref[0, r : r + 1, lanes] = ending


def first_part(
    channels,
    place_ref,
    squares_ref,
    before_ref,
    ids_ref,
    table_ref,
    gain_ref,
    filters_ref,
    rates_ref,
    forward_ref,
    spectrum_ref,
    back_ref,
    state_ref,
    kept_ref,
    ext_ref,
    gated_ref,
    query_ref,
    mixed_ref,
    forward_v,
    back_v,
    sems,
):
    loads = [
        pltpu.make_async_copy(forward_ref, forward_v, sems.at[0]),
        pltpu.make_async_copy(back_ref, back_v, sems.at[1]),
    ]
    for load in loads:
        load.start()
    vocab, width = table_ref.shape
    modes = rates_ref.shape[0]
    stage = Stage(width, modes, kept_ref, ext_ref, gated_ref, query_ref, mixed_ref)
    before = before_ref[:, before_ref.shape[1] - HALO_IDS :]
    hot = one_hot(place_ref[0], before, ids_ref[...], vocab)
    inverse = lax.rsqrt(jnp.sum(squares_ref[...], axis=0) / channels + 1e-06)
    column = jnp.transpose(jnp.broadcast_to(inverse, (8, vocab)))[:, 0:1]
    scaled = (table_ref[...].astype(F32) * column * gain_ref[...]).astype(BF16)
    main = HALO_STEPS + SPAN

    def loop(body):
        def step(i, carry):
            body(i)
            return carry

        lax.fori_loop(0, STEPS // BLOCK, step, 0)

    stage.embed(hot, scaled)
    stage.edges(filters_ref)

    def convolve(i):
        stage.gate(filters_ref, main + i * BLOCK, BLOCK)
        stage.ask(filters_ref, main + i * BLOCK, BLOCK)

    loop(convolve)
    loads[0].wait()
    stage.forward(forward_v, spectrum_ref)
    loads[1].wait()
    stage.backward(back_v)
    loop(lambda i: stage.drive(filters_ref, i))
    zero = jnp.zeros((LINES, LANES), F32)
    for g in range(stage.count):
        decays = stage.decays(rates_ref, g)

        def gather(i, states, g=g, decays=decays):
            return stage.absorb(decays, states, i, g)

        states = lax.fori_loop(0, STEPS // BLOCK, gather, (zero,) * modes)
        stage.settle(rates_ref, state_ref, states, g)
    for k in range(1, state_ref.shape[0]):
        state_ref[k] = state_ref[0]


def coefficients(rates, residues):
    double = 2.0 * rates
    series = double * (1.0 + double * (-0.5 + double * (1.0 / 6 + double * (-1.0 / 24))))
    return residues * jnp.sqrt(jnp.where(double < 0.02, series, 1.0 - jnp.exp(-double)))


def near_part(place_ref, rows_ref, rates_ref, near_ref, total_ref):
    across = jnp.exp(-rates_ref[...] * (1.0 * STEPS * LINES))
    own = lax.rem(place_ref[0], rows_ref.shape[0])
    total = jnp.zeros(rates_ref.shape, F32)
    near = total
    for j in range(rows_ref.shape[0]):
        near = jnp.where(own == j, total, near)
        total = across * total + rows_ref[j].astype(F32)
    near_ref[...] = near
    total_ref[...] = jnp.broadcast_to(total.astype(BF16)[None], total_ref.shape)


def second_part(
    filters_ref,
    rates_ref,
    residues_ref,
    kept_ref,
    order_ref,
    query_ref,
    whole_ref,
    weights_ref,
    query_v,
    whole_v,
    order_v,
    sems,
):
    load = pltpu.make_async_copy(order_ref, order_v, sems.at[0])
    load.start()
    weights_ref[...] = coefficients(rates_ref[...], residues_ref[...])
    modes, width = rates_ref.shape
    groups = width // LANES
    index = lax.broadcasted_iota(jnp.int32, (LINES, LANES), 0)
    second_ref, driven_ref, endings_ref = parts_of(kept_ref, modes)
    for group in range(groups):
        taps = taps_of(filters_ref, 1, 0, group)

        def conv_query(b, carry, group=group, taps=taps):
            window = second_window(second_ref, b, group)
            rows = pl.ds(pl.multiple_of(b * BLOCK * LINES, BLOCK * LINES), BLOCK * LINES)
            query_v[rows, lanes_of(group)] = (
                tapped(window, taps, BLOCK).reshape(BLOCK * LINES, LANES).astype(BF16)
            )
            return carry

        lax.fori_loop(0, STEPS // BLOCK, conv_query, 0)

        decays, weights, starts = [], [], []
        for r in range(modes):
            rate = jnp.broadcast_to(rates_ref[r : r + 1, lanes_of(group)], (LINES, LANES))
            ending = endings_ref[r * 2 * LINES : (r + 1) * 2 * LINES, lanes_of(group)].astype(F32)
            total = ending[:LINES] + ending[LINES:]
            for k in (1, 2, 4):
                moved = jnp.where(index >= k, pltpu.roll(total, k, 0), 0.0)
                total = total + jnp.exp(-rate * (1.0 * STEPS * k)) * moved
            starts.append(jnp.where(index >= 1, pltpu.roll(total, 1, 0), 0.0))
            decays.append(jnp.exp(-rate))
            weights.append(
                jnp.broadcast_to(weights_ref[r : r + 1, lanes_of(group)], (LINES, LANES))
            )

        def respond(b, states, group=group, decays=decays, weights=weights):
            values = driven_steps(driven_ref, b, group)
            outs = []
            for k in range(BLOCK):
                states = tuple(d * s + values[k] for d, s in zip(decays, states))
                sums = [w * s for w, s in zip(weights, states)]
                while len(sums) > 1:
                    sums = [a + b for a, b in zip(sums[0::2], sums[1::2])]
                outs.append(sums[0])
            rows = pl.ds(pl.multiple_of(b * BLOCK * LINES, BLOCK * LINES), BLOCK * LINES)
            whole_v[rows, lanes_of(group)] = jnp.concatenate(outs, 0)
            return states

        lax.fori_loop(0, STEPS // BLOCK, respond, tuple(starts))
    load.wait()
    query_ref[...] = jnp.dot(
        order_v[...], query_v[...], preferred_element_type=F32
    ).astype(BF16)
    high, low = halves(whole_v[...])
    whole_ref[...] = jnp.dot(order_v[...], high, preferred_element_type=F32) + jnp.dot(
        order_v[...], low, preferred_element_type=F32
    )


def third_part(
    inner,
    place_ref,
    near_ref,
    totals_ref,
    rates_ref,
    weights_ref,
    query_ref,
    whole_ref,
    out_ref,
    result_v,
    sems,
):
    modes, width = rates_ref.shape
    groups = width // LANES
    span = 1.0 * STEPS * LINES
    across = jnp.exp(-rates_ref[...] * (span * inner))
    own = lax.rem(place_ref[0], inner)
    rank = lax.div(place_ref[0], inner)
    far = jnp.zeros(rates_ref.shape, F32)
    last = totals_ref.shape[0] - 1
    for j in range(last + 1):
        far = jnp.where(j < rank, across * far + totals_ref[last - j].astype(F32), far)
    incoming = near_ref[...] + jnp.exp(-rates_ref[...] * (span * own.astype(F32))) * far

    stores = []
    across = jnp.exp(-rates_ref[...] * LINES)
    entering = weights_ref[...] * incoming
    line = lax.broadcasted_iota(jnp.int32, (LINES, LANES), 0).astype(F32)
    for group in range(groups):
        decays, terms = [], []
        for r in range(modes):
            decays.append(jnp.broadcast_to(across[r : r + 1, lanes_of(group)], (LINES, LANES)))
            rise = jnp.exp(-rates_ref[r : r + 1, lanes_of(group)] * (line + 1.0))
            terms.append(rise * entering[r : r + 1, lanes_of(group)])

        def lift(b, terms, group=group, decays=decays):
            rows = pl.ds(pl.multiple_of(b * 64, 64), 64)
            outs = []
            for k in range(8):
                sums = list(terms)
                while len(sums) > 1:
                    sums = [a + b for a, b in zip(sums[0::2], sums[1::2])]
                outs.append(sums[0])
                terms = tuple(t * d for t, d in zip(terms, decays))
            whole = whole_ref[rows, lanes_of(group)] + jnp.concatenate(outs, 0)
            query = query_ref[rows, lanes_of(group)].astype(F32)
            result_v[rows, lanes_of(group)] = (query * whole).astype(BF16)
            return terms

        lax.fori_loop(0, STEPS // 8, lift, tuple(terms))
        stores.append(
            pltpu.make_async_copy(
                result_v.at[:, lanes_of(group)], out_ref.at[:, lanes_of(group)], sems.at[group]
            )
        )
        stores[-1].start()
    for store in stores:
        store.wait()


VMEM = pl.BlockSpec(memory_space=pltpu.VMEM)
SMEM = pl.BlockSpec(memory_space=pltpu.SMEM)
HBM = pl.BlockSpec(memory_space=pl.ANY)


FAR = pl.BlockSpec(memory_space=pltpu.HBM)


def far(array):
    return pltpu.with_memory_space_constraint(jnp.asarray(array), pltpu.HBM)


def cost(flops, moved):
    return pl.CostEstimate(flops=int(flops), bytes_accessed=int(moved), transcendentals=0)


def call(
    kernel, name, ins, outs, scratch=(), sems=0, out_space=None, limit=24, flops=1e9, moved=4e6
):
    return pl.pallas_call(
        kernel,
        name=name,
        in_specs=ins,
        out_specs=[out_space or VMEM] * len(outs),
        out_shape=[jax.ShapeDtypeStruct(*o) for o in outs],
        scratch_shapes=[pltpu.VMEM(*s) for s in scratch]
        + ([pltpu.SemaphoreType.DMA((sems,))] if sems else []),
        compiler_params=pltpu.CompilerParams(vmem_limit_bytes=limit << 20),
        cost_estimate=cost(flops, moved),
    )


def local(
    token_ids, embed_table, norm_gain, short_filters, medium_filter, mode_rates, mode_residues
):
    vocab, width = embed_table.shape
    count = token_ids.shape[0]
    modes = mode_rates.shape[0]
    taps = medium_filter.shape[0]
    shards = lax.axis_size("ch")
    length = lax.axis_size("seq")
    inner = min(INNER, length)
    near_groups = [[o * inner + i for i in range(inner)] for o in range(length // inner)]
    far_groups = [[o * inner + i for o in reversed(range(length // inner))] for i in range(inner)]
    const = tables(taps)
    place = jnp.reshape(lax.axis_index("seq").astype(jnp.int32), (1,))

    before = lax.ppermute(token_ids, "seq", [(i, i + 1) for i in range(length - 1)])
    (partial,) = call(
        square_sums, "square_sums", [VMEM], [((shards, 1, vocab), F32)], limit=8
    )(embed_table)
    squares = lax.all_to_all(partial, "ch", 0, 0)
    (spectrum,) = call(
        spectrum_of, "spectrum_of", [VMEM] * 2, [((FREQS, width), F32)], limit=8
    )(const["taps_wave"], medium_filter)
    kept_shape = (SECOND_ROWS + STEPS * LINES + 2 * modes * LINES, width)
    state, kept = call(
        functools.partial(first_part, channels_of(width, shards)),
        "first_part",
        [SMEM] + [VMEM] * 7 + [FAR, VMEM, FAR],
        [((inner, modes, width), BF16), (kept_shape, BF16)],
        [
            ((EXT_STEPS, LINES, width), F32),
            ((OUT_STEPS * LINES, width), BF16),
            ((OUT_STEPS, LINES, width), F32),
            ((FREQS, width), BF16),
            (const["forward"].shape, BF16),
            (const["back"].shape, BF16),
        ],
        sems=2,
    )(
        place,
        squares,
        before[None],
        token_ids[None],
        embed_table,
        norm_gain[None],
        short_filters,
        mode_rates,
        far(const["forward"]),
        spectrum,
        far(const["back"]),
    )
    rows = lax.all_to_all(state, "seq", 0, 0, axis_index_groups=near_groups, tiled=True)
    query, whole, weights = call(
        second_part,
        "second_part",
        [VMEM] * 4 + [FAR],
        [((count, width), BF16), ((count, width), F32), ((modes, width), F32)],
        [((count, width), BF16), ((count, width), F32), ((count, count), BF16)],
        sems=1,
        flops=4e9,
        moved=1e7,
    )(short_filters, mode_rates, mode_residues, kept, far(const["order"]))
    near, totals = call(
        near_part,
        "near_part",
        [SMEM] + [VMEM] * 2,
        [((modes, width), F32), ((length // inner, modes, width), BF16)],
        limit=4,
    )(place, rows, mode_rates)
    totals = lax.all_to_all(totals, "seq", 0, 0, axis_index_groups=far_groups, tiled=True)
    (out,) = call(
        functools.partial(third_part, inner),
        "third_part",
        [SMEM] + [VMEM] * 6,
        [((count, width), BF16)],
        [((count, width), BF16)],
        sems=width // LANES,
        out_space=HBM,
        limit=12,
    )(place, near, totals, mode_rates, weights, query, whole)
    return out


def channels_of(width, shards):
    return width * shards


def solution(mesh):
    placed = (
        P("seq"),
        P(None, "ch"),
        P("ch"),
        P(None, None, None, "ch"),
        P(None, "ch"),
        P(None, "ch"),
        P(None, "ch"),
    )
    return jax.shard_map(
        local, mesh=mesh, in_specs=placed, out_specs=P("seq", "ch"), check_vma=False
    )
```

```python
import functools

import jax
import jax.numpy as jnp
import ml_dtypes
import numpy as np
from jax import lax
from jax.experimental import pallas as pl
from jax.experimental.pallas import tpu as pltpu
from jax.sharding import PartitionSpec as P

F32 = jnp.float32
BF16 = jnp.bfloat16
LANES = 128
STEPS = 64
LINES = 8
HALO_STEPS = 18
SPAN = 6
EXT_STEPS = SPAN + HALO_STEPS + SPAN + STEPS
OUT_STEPS = EXT_STEPS - SPAN
HALO_IDS = 256
BLOCK = 16
SECOND_ROWS = (SPAN + STEPS) * LINES
FREQS = 656
INNER = 8
NT = (((1,), (1,)), ((), ()))


def step_times():
    lines = np.arange(LINES)
    halo = -HALO_STEPS * LINES + lines[None] * HALO_STEPS + np.arange(-SPAN, HALO_STEPS)[:, None]
    main = lines[None] * STEPS + np.arange(-SPAN, STEPS)[:, None]
    return np.concatenate([halo, main], 0)


def tables(taps):
    times = step_times()
    pair = np.arange(FREQS)
    freq = (pair // 16) * 8 + pair % 8 + 0.5
    quarter = np.where(pair % 16 < 8, 0.0, 0.25)
    origin = HALO_STEPS * LINES

    def wave(position):
        return np.cos(2 * np.pi * (np.outer(freq, position) / FREQS + quarter[:, None]))

    used = times[SPAN:].copy()
    valid = np.ones(used.shape, bool)
    valid[HALO_STEPS : HALO_STEPS + SPAN] = False
    valid &= used >= -(taps - 1 + SPAN)
    forward = wave((used + origin).reshape(-1)) * valid.reshape(1, -1)
    taps_wave = wave(np.arange(taps))
    halo_rows = times[SPAN + HALO_STEPS - SPAN : SPAN + HALO_STEPS].reshape(-1)
    main_rows = times[SPAN + HALO_STEPS + SPAN :].reshape(-1)
    back = wave(np.concatenate([halo_rows, main_rows]) + origin).T * (2.0 / FREQS)
    order = np.zeros((STEPS * LINES, STEPS * LINES), np.float32)
    order[main_rows, np.arange(main_rows.size)] = 1.0
    half = lambda a: np.asarray(a, np.float32).astype(ml_dtypes.bfloat16)
    return dict(
        forward=half(forward),
        taps_wave=split_wave(taps_wave),
        back=half(back),
        order=half(order),
    )


def split_wave(wave):
    high = np.asarray(wave, np.float32).astype(ml_dtypes.bfloat16)
    low = (wave - high.astype(np.float64)).astype(ml_dtypes.bfloat16)
    return np.concatenate([high, low, high], 1)


def lanes_of(group):
    return slice(group * LANES, (group + 1) * LANES)


def halves(values):
    high = values.astype(BF16)
    return high, (values - high.astype(F32)).astype(BF16)


def square_sums(table_ref, sums_ref):
    table = table_ref[...].astype(F32)
    high, low = halves(table * table)
    ones = jnp.ones((8, table.shape[1]), BF16)
    total = lax.dot_general(ones, high, NT, preferred_element_type=F32)
    total += lax.dot_general(ones, low, NT, preferred_element_type=F32)
    sums_ref[...] = jnp.broadcast_to(total[None, :1], sums_ref.shape)


def spectrum_of(wave_ref, medium_ref, spectrum_ref):
    high, low = halves(medium_ref[...])
    spectrum_ref[...] = jnp.dot(
        wave_ref[...], jnp.concatenate([high, high, low], 0), preferred_element_type=F32
    )


def one_hot(place, before, own, vocab):
    def digits(ids):
        high = lax.shift_right_arithmetic(ids, 4)
        low = ids - high * 16
        row = lax.broadcasted_iota(jnp.int32, (8, ids.shape[1]), 0)
        return jnp.where(row == 0, high, jnp.where(row == 1, low, 0)).astype(F32).astype(BF16)

    def picked(ids, first, steps, spread, shift):
        rows = steps * LINES
        row = lax.broadcasted_iota(jnp.int32, (rows, 1), 0)
        step = lax.shift_right_logical(row, 3)
        time = lax.bitwise_and(row, LINES - 1) * spread + step + shift
        column = lax.broadcasted_iota(jnp.int32, (rows, ids.shape[1]), 1) + first
        pick = jnp.where(column == time, 1.0, 0.0).astype(BF16)
        return lax.dot_general(pick, digits(ids), NT, preferred_element_type=F32)

    before = jnp.where(place > 0, before, -1)
    halo = picked(before, -HALO_IDS, SPAN + HALO_STEPS, HALO_STEPS, -LINES * HALO_STEPS - SPAN)
    edge = picked(before, -HALO_IDS, SPAN, STEPS, -SPAN)
    main = picked(own, 0, SPAN + STEPS, STEPS, -SPAN)
    column = jnp.concatenate([halo, edge + main[: SPAN * LINES], main[SPAN * LINES :]], 0)
    ids = (column[:, 0:1] * 16.0 + column[:, 1:2]).astype(jnp.int32)
    hot = ids == lax.broadcasted_iota(jnp.int32, (column.shape[0], vocab), 1)
    return jnp.where(hot, 1.0, 0.0).astype(BF16)


def taps_of(filters_ref, block, stream, group):
    return [
        jnp.broadcast_to(filters_ref[block, stream, d : d + 1, lanes_of(group)], (LINES, LANES))
        for d in range(SPAN + 1)
    ]


def tapped(window, taps, rows):
    total = None
    for d, tap in enumerate(taps):
        term = window[SPAN - d : SPAN - d + rows] * tap[None]
        total = term if total is None else total + term
    return total


def rows_at(start, size):
    return pl.ds(start if isinstance(start, int) else pl.multiple_of(start, 16), size)


def second_window(second_ref, b, group):
    rows = rows_at(b * BLOCK * LINES, (BLOCK + SPAN) * LINES)
    return second_ref[rows, lanes_of(group)].astype(F32).reshape(BLOCK + SPAN, LINES, LANES)


def driven_steps(driven_ref, b, group):
    rows = rows_at(b * BLOCK * LINES, BLOCK * LINES)
    return driven_ref[rows, lanes_of(group)].astype(F32).reshape(BLOCK, LINES, LANES)


def parts_of(kept_ref, modes):
    return (
        kept_ref.at[pl.ds(0, SECOND_ROWS)],
        kept_ref.at[pl.ds(SECOND_ROWS, STEPS * LINES)],
        kept_ref.at[pl.ds(SECOND_ROWS + STEPS * LINES, 2 * modes * LINES)],
    )


class Stage:
    def __init__(self, width, modes, kept_ref, ext_ref, gated_ref, query_ref, mixed_ref):
        self.width, self.modes = width, modes
        self.count = width // LANES
        self.second, self.driven, self.endings = parts_of(kept_ref, modes)
        self.ext, self.gated, self.query, self.mixed = ext_ref, gated_ref, query_ref, mixed_ref

    def embed(self, hot, scaled):
        rows = jnp.dot(hot, scaled, preferred_element_type=F32)
        self.ext[...] = rows.reshape(EXT_STEPS, LINES, self.width)

    def gate(self, filters_ref, at, steps):
        for g in range(self.count):
            window = self.ext[pl.ds(at, steps + SPAN), :, lanes_of(g)]
            key, value = [
                tapped(window, taps_of(filters_ref, 0, s, g), steps)
                for s in (1, 2)
            ]
            self.gated[rows_at(at * LINES, steps * LINES), lanes_of(g)] = (
                (key * value).reshape(steps * LINES, LANES).astype(BF16)
            )

    def ask(self, filters_ref, at, steps):
        for g in range(self.count):
            window = self.ext[pl.ds(at, steps + SPAN), :, lanes_of(g)]
            taps = taps_of(filters_ref, 0, 0, g)
            self.query[pl.ds(at, steps), :, lanes_of(g)] = tapped(window, taps, steps)

    def edges(self, filters_ref):
        gap = slice(HALO_STEPS * LINES, (HALO_STEPS + SPAN) * LINES)
        self.gated[gap, :] = jnp.zeros((SPAN * LINES, self.width), BF16)
        self.gate(filters_ref, 0, HALO_STEPS)
        self.ask(filters_ref, HALO_STEPS - SPAN, SPAN)

    def forward(self, forward_ref, spectrum_ref):
        wave = jnp.dot(forward_ref[...], self.gated[...], preferred_element_type=F32)
        wave = wave.reshape(FREQS // 16, 16, self.width)
        shape = spectrum_ref[...].reshape(FREQS // 16, 16, self.width)
        real, imag = wave[:, :8], wave[:, 8:]
        real_h, imag_h = shape[:, :8], shape[:, 8:]
        product = jnp.concatenate(
            [real * real_h - imag * imag_h, real * imag_h + imag * real_h], axis=1
        )
        self.mixed[...] = product.reshape(FREQS, self.width).astype(BF16)

    def backward(self, back_ref):
        middle = jnp.dot(back_ref[...], self.mixed[...], preferred_element_type=F32)
        middle = middle.reshape(SPAN + STEPS, LINES, self.width)
        halo = middle[:SPAN] * self.query[HALO_STEPS - SPAN : HALO_STEPS]
        halo = halo.astype(BF16).astype(F32)
        main = middle[SPAN:] * self.query[HALO_STEPS + SPAN :]
        main = main.reshape(STEPS * LINES, self.width).astype(BF16)
        self.second[SPAN * LINES :, :] = main
        last = main[(STEPS - SPAN) * LINES :].astype(F32).reshape(SPAN, LINES, self.width)
        first = []
        for k in range(SPAN):
            own = pltpu.roll(last[k], 1, 0)
            other = pltpu.roll(halo[k], 1, 0)
            line = lax.broadcasted_iota(jnp.int32, own.shape, 0)
            first.append(jnp.where(line == 0, other, own))
        self.second[: SPAN * LINES, :] = jnp.concatenate(first, 0).astype(BF16)

    def drive(self, filters_ref, b):
        for g in range(self.count):
            window = second_window(self.second, b, g)
            key, value = [
                tapped(window, taps_of(filters_ref, 1, s, g), BLOCK)
                for s in (1, 2)
            ]
            self.driven[rows_at(b * BLOCK * LINES, BLOCK * LINES), lanes_of(g)] = (
                (key * value).reshape(BLOCK * LINES, LANES).astype(BF16)
            )

    def decays(self, rates_ref, g):
        lanes = lanes_of(g)
        return [
            jnp.exp(-jnp.broadcast_to(rates_ref[r : r + 1, lanes], (LINES, LANES)))
            for r in range(self.modes)
        ]

    def absorb(self, decays, states, b, g):
        values = driven_steps(self.driven, b, g)
        for k in range(BLOCK):
            states = tuple(d * s + values[k] for d, s in zip(decays, states))
        return states

    def settle(self, rates_ref, state_ref, states, g):
        lanes = lanes_of(g)
        line = lax.broadcasted_iota(jnp.int32, (LINES, LANES), 0).astype(F32)
        for r in range(self.modes):
            self.endings[r * 2 * LINES : (r + 1) * 2 * LINES, lanes_of(g)] = jnp.concatenate(
                [h.astype(F32) for h in halves(states[r])], 0
            ).astype(BF16)
            weight = jnp.exp(-rates_ref[r : r + 1, lanes] * ((LINES - 1.0 - line) * STEPS))
            ending = jnp.sum(states[r] * weight, axis=0, keepdims=True).astype(state_ref.dtype)
            state_ref[0, r : r + 1, lanes] = ending


def first_part(
    channels,
    place_ref,
    squares_ref,
    before_ref,
    ids_ref,
    table_ref,
    gain_ref,
    filters_ref,
    rates_ref,
    forward_ref,
    spectrum_ref,
    back_ref,
    state_ref,
    kept_ref,
    ext_ref,
    gated_ref,
    query_ref,
    mixed_ref,
    forward_v,
    back_v,
    sems,
):
    loads = [
        pltpu.make_async_copy(forward_ref, forward_v, sems.at[0]),
        pltpu.make_async_copy(back_ref, back_v, sems.at[1]),
    ]
    for load in loads:
        load.start()
    vocab, width = table_ref.shape
    modes = rates_ref.shape[0]
    stage = Stage(width, modes, kept_ref, ext_ref, gated_ref, query_ref, mixed_ref)
    before = before_ref[:, before_ref.shape[1] - HALO_IDS :]
    hot = one_hot(place_ref[0], before, ids_ref[...], vocab)
    inverse = lax.rsqrt(jnp.sum(squares_ref[...], axis=0) / channels + 1e-06)
    column = jnp.transpose(jnp.broadcast_to(inverse, (8, vocab)))[:, 0:1]
    scaled = (table_ref[...].astype(F32) * column * gain_ref[...]).astype(BF16)
    main = HALO_STEPS + SPAN

    def loop(body):
        def step(i, carry):
            body(i)
            return carry

        lax.fori_loop(0, STEPS // BLOCK, step, 0)

    stage.embed(hot, scaled)
    stage.edges(filters_ref)

    def convolve(i):
        stage.gate(filters_ref, main + i * BLOCK, BLOCK)
        stage.ask(filters_ref, main + i * BLOCK, BLOCK)

    loop(convolve)
    loads[0].wait()
    stage.forward(forward_v, spectrum_ref)
    loads[1].wait()
    stage.backward(back_v)
    loop(lambda i: stage.drive(filters_ref, i))
    zero = jnp.zeros((LINES, LANES), F32)
    for g in range(stage.count):
        decays = stage.decays(rates_ref, g)

        def gather(i, states, g=g, decays=decays):
            return stage.absorb(decays, states, i, g)

        states = lax.fori_loop(0, STEPS // BLOCK, gather, (zero,) * modes)
        stage.settle(rates_ref, state_ref, states, g)
    for k in range(1, state_ref.shape[0]):
        state_ref[k] = state_ref[0]


def coefficients(rates, residues):
    double = 2.0 * rates
    series = double * (1.0 + double * (-0.5 + double * (1.0 / 6 + double * (-1.0 / 24))))
    return residues * jnp.sqrt(jnp.where(double < 0.02, series, 1.0 - jnp.exp(-double)))


def near_order(inner):
    late = inner // 2
    order = [late]
    for step in range(late):
        order += [place for place in (step, inner - step) if place % inner not in order and place < inner]
    order += [place for place in range(inner) if place not in order]
    return order[:0:-1] + order[:1]


def near_part(place_ref, rows_ref, rates_ref, near_ref, total_ref):
    across = jnp.exp(-rates_ref[...] * (1.0 * STEPS * LINES))
    own = lax.rem(place_ref[0], rows_ref.shape[0])
    total = jnp.zeros(rates_ref.shape, F32)
    near = total
    order = near_order(rows_ref.shape[0])
    for j in range(rows_ref.shape[0]):
        near = jnp.where(own == j, total, near)
        total = across * total + rows_ref[order.index(j)].astype(F32)
    near_ref[...] = near
    total_ref[...] = jnp.broadcast_to(total.astype(BF16)[None], total_ref.shape)


def second_part(
    filters_ref,
    rates_ref,
    residues_ref,
    kept_ref,
    order_ref,
    query_ref,
    whole_ref,
    weights_ref,
    query_v,
    whole_v,
    order_v,
    sems,
):
    load = pltpu.make_async_copy(order_ref, order_v, sems.at[0])
    load.start()
    weights_ref[...] = coefficients(rates_ref[...], residues_ref[...])
    modes, width = rates_ref.shape
    groups = width // LANES
    index = lax.broadcasted_iota(jnp.int32, (LINES, LANES), 0)
    second_ref, driven_ref, endings_ref = parts_of(kept_ref, modes)
    for group in range(groups):
        taps = taps_of(filters_ref, 1, 0, group)

        def conv_query(b, carry, group=group, taps=taps):
            window = second_window(second_ref, b, group)
            rows = pl.ds(pl.multiple_of(b * BLOCK * LINES, BLOCK * LINES), BLOCK * LINES)
            query_v[rows, lanes_of(group)] = (
                tapped(window, taps, BLOCK).reshape(BLOCK * LINES, LANES).astype(BF16)
            )
            return carry

        lax.fori_loop(0, STEPS // BLOCK, conv_query, 0)

        decays, weights, starts = [], [], []
        for r in range(modes):
            rate = jnp.broadcast_to(rates_ref[r : r + 1, lanes_of(group)], (LINES, LANES))
            ending = endings_ref[r * 2 * LINES : (r + 1) * 2 * LINES, lanes_of(group)].astype(F32)
            total = ending[:LINES] + ending[LINES:]
            for k in (1, 2, 4):
                moved = jnp.where(index >= k, pltpu.roll(total, k, 0), 0.0)
                total = total + jnp.exp(-rate * (1.0 * STEPS * k)) * moved
            starts.append(jnp.where(index >= 1, pltpu.roll(total, 1, 0), 0.0))
            decays.append(jnp.exp(-rate))
            weights.append(
                jnp.broadcast_to(weights_ref[r : r + 1, lanes_of(group)], (LINES, LANES))
            )

        def respond(b, states, group=group, decays=decays, weights=weights):
            values = driven_steps(driven_ref, b, group)
            outs = []
            for k in range(BLOCK):
                states = tuple(d * s + values[k] for d, s in zip(decays, states))
                sums = [w * s for w, s in zip(weights, states)]
                while len(sums) > 1:
                    sums = [a + b for a, b in zip(sums[0::2], sums[1::2])]
                outs.append(sums[0])
            rows = pl.ds(pl.multiple_of(b * BLOCK * LINES, BLOCK * LINES), BLOCK * LINES)
            whole_v[rows, lanes_of(group)] = jnp.concatenate(outs, 0)
            return states

        lax.fori_loop(0, STEPS // BLOCK, respond, tuple(starts))
    load.wait()
    query_ref[...] = jnp.dot(
        order_v[...], query_v[...], preferred_element_type=F32
    ).astype(BF16)
    high, low = halves(whole_v[...])
    whole_ref[...] = jnp.dot(order_v[...], high, preferred_element_type=F32) + jnp.dot(
        order_v[...], low, preferred_element_type=F32
    )


def third_part(
    inner,
    place_ref,
    near_ref,
    totals_ref,
    rates_ref,
    weights_ref,
    query_ref,
    whole_ref,
    out_ref,
    result_v,
    sems,
):
    modes, width = rates_ref.shape
    groups = width // LANES
    span = 1.0 * STEPS * LINES
    across = jnp.exp(-rates_ref[...] * (span * inner))
    own = lax.rem(place_ref[0], inner)
    rank = lax.div(place_ref[0], inner)
    far = jnp.zeros(rates_ref.shape, F32)
    last = totals_ref.shape[0] - 1
    for j in range(last + 1):
        far = jnp.where(j < rank, across * far + totals_ref[last - j].astype(F32), far)
    incoming = near_ref[...] + jnp.exp(-rates_ref[...] * (span * own.astype(F32))) * far

    stores = []
    across = jnp.exp(-rates_ref[...] * LINES)
    entering = weights_ref[...] * incoming
    line = lax.broadcasted_iota(jnp.int32, (LINES, LANES), 0).astype(F32)
    for group in range(groups):
        decays, terms = [], []
        for r in range(modes):
            decays.append(jnp.broadcast_to(across[r : r + 1, lanes_of(group)], (LINES, LANES)))
            rise = jnp.exp(-rates_ref[r : r + 1, lanes_of(group)] * (line + 1.0))
            terms.append(rise * entering[r : r + 1, lanes_of(group)])

        def lift(b, terms, group=group, decays=decays):
            rows = pl.ds(pl.multiple_of(b * 64, 64), 64)
            outs = []
            for k in range(8):
                sums = list(terms)
                while len(sums) > 1:
                    sums = [a + b for a, b in zip(sums[0::2], sums[1::2])]
                outs.append(sums[0])
                terms = tuple(t * d for t, d in zip(terms, decays))
            whole = whole_ref[rows, lanes_of(group)] + jnp.concatenate(outs, 0)
            query = query_ref[rows, lanes_of(group)].astype(F32)
            result_v[rows, lanes_of(group)] = (query * whole).astype(BF16)
            return terms

        lax.fori_loop(0, STEPS // 8, lift, tuple(terms))
        stores.append(
            pltpu.make_async_copy(
                result_v.at[:, lanes_of(group)], out_ref.at[:, lanes_of(group)], sems.at[group]
            )
        )
        stores[-1].start()
    for store in stores:
        store.wait()


VMEM = pl.BlockSpec(memory_space=pltpu.VMEM)
SMEM = pl.BlockSpec(memory_space=pltpu.SMEM)
HBM = pl.BlockSpec(memory_space=pl.ANY)


FAR = pl.BlockSpec(memory_space=pltpu.HBM)


def far(array):
    return pltpu.with_memory_space_constraint(jnp.asarray(array), pltpu.HBM)


def cost(flops, moved):
    return pl.CostEstimate(flops=int(flops), bytes_accessed=int(moved), transcendentals=0)


def call(
    kernel, name, ins, outs, scratch=(), sems=0, out_space=None, limit=24, flops=1e9, moved=4e6
):
    return pl.pallas_call(
        kernel,
        name=name,
        in_specs=ins,
        out_specs=[out_space or VMEM] * len(outs),
        out_shape=[jax.ShapeDtypeStruct(*o) for o in outs],
        scratch_shapes=[pltpu.VMEM(*s) for s in scratch]
        + ([pltpu.SemaphoreType.DMA((sems,))] if sems else []),
        compiler_params=pltpu.CompilerParams(vmem_limit_bytes=limit << 20),
        cost_estimate=cost(flops, moved),
    )


def local(
    token_ids, embed_table, norm_gain, short_filters, medium_filter, mode_rates, mode_residues
):
    vocab, width = embed_table.shape
    count = token_ids.shape[0]
    modes = mode_rates.shape[0]
    taps = medium_filter.shape[0]
    shards = lax.axis_size("ch")
    length = lax.axis_size("seq")
    inner = min(INNER, length)
    near_groups = [[o * inner + i for i in near_order(inner)] for o in range(length // inner)]
    far_groups = [[o * inner + i for o in reversed(range(length // inner))] for i in range(inner)]
    const = tables(taps)
    place = jnp.reshape(lax.axis_index("seq").astype(jnp.int32), (1,))

    before = lax.ppermute(token_ids, "seq", [(i, i + 1) for i in range(length - 1)])
    (partial,) = call(
        square_sums, "square_sums", [VMEM], [((shards, 1, vocab), F32)], limit=8
    )(embed_table)
    squares = lax.all_to_all(partial, "ch", 0, 0)
    (spectrum,) = call(
        spectrum_of, "spectrum_of", [VMEM] * 2, [((FREQS, width), F32)], limit=8
    )(const["taps_wave"], medium_filter)
    kept_shape = (SECOND_ROWS + STEPS * LINES + 2 * modes * LINES, width)
    state, kept = call(
        functools.partial(first_part, channels_of(width, shards)),
        "first_part",
        [SMEM] + [VMEM] * 7 + [FAR, VMEM, FAR],
        [((inner, modes, width), BF16), (kept_shape, BF16)],
        [
            ((EXT_STEPS, LINES, width), F32),
            ((OUT_STEPS * LINES, width), BF16),
            ((OUT_STEPS, LINES, width), F32),
            ((FREQS, width), BF16),
            (const["forward"].shape, BF16),
            (const["back"].shape, BF16),
        ],
        sems=2,
    )(
        place,
        squares,
        before[None],
        token_ids[None],
        embed_table,
        norm_gain[None],
        short_filters,
        mode_rates,
        far(const["forward"]),
        spectrum,
        far(const["back"]),
    )
    rows = lax.all_to_all(state, "seq", 0, 0, axis_index_groups=near_groups, tiled=True)
    query, whole, weights = call(
        second_part,
        "second_part",
        [VMEM] * 4 + [FAR],
        [((count, width), BF16), ((count, width), F32), ((modes, width), F32)],
        [((count, width), BF16), ((count, width), F32), ((count, count), BF16)],
        sems=1,
        flops=4e9,
        moved=1e7,
    )(short_filters, mode_rates, mode_residues, kept, far(const["order"]))
    near, totals = call(
        near_part,
        "near_part",
        [SMEM] + [VMEM] * 2,
        [((modes, width), F32), ((length // inner, modes, width), BF16)],
        limit=4,
    )(place, rows, mode_rates)
    totals = lax.all_to_all(totals, "seq", 0, 0, axis_index_groups=far_groups, tiled=True)
    (out,) = call(
        functools.partial(third_part, inner),
        "third_part",
        [SMEM] + [VMEM] * 6,
        [((count, width), BF16)],
        [((count, width), BF16)],
        sems=width // LANES,
        out_space=HBM,
        limit=12,
    )(place, near, totals, mode_rates, weights, query, whole)
    return out


def channels_of(width, shards):
    return width * shards


def solution(mesh):
    placed = (
        P("seq"),
        P(None, "ch"),
        P("ch"),
        P(None, None, None, "ch"),
        P(None, "ch"),
        P(None, "ch"),
        P(None, "ch"),
    )
    return jax.shard_map(
        local, mesh=mesh, in_specs=placed, out_specs=P("seq", "ch"), check_vma=False
    )
```

```python
import functools

import jax
import jax.numpy as jnp
import ml_dtypes
import numpy as np
from jax import lax
from jax.experimental import pallas as pl
from jax.experimental.pallas import tpu as pltpu
from jax.sharding import PartitionSpec as P

F32 = jnp.float32
BF16 = jnp.bfloat16
LANES = 128
STEPS = 64
LINES = 8
HALO_STEPS = 18
SPAN = 6
EXT_STEPS = SPAN + HALO_STEPS + SPAN + STEPS
OUT_STEPS = EXT_STEPS - SPAN
HALO_IDS = 256
BLOCK = 16
SECOND_ROWS = (SPAN + STEPS) * LINES
FREQS = 656
INNER = 8
NT = (((1,), (1,)), ((), ()))


def step_times():
    lines = np.arange(LINES)
    halo = -HALO_STEPS * LINES + lines[None] * HALO_STEPS + np.arange(-SPAN, HALO_STEPS)[:, None]
    main = lines[None] * STEPS + np.arange(-SPAN, STEPS)[:, None]
    return np.concatenate([halo, main], 0)


def tables(taps):
    times = step_times()
    pair = np.arange(FREQS)
    freq = (pair // 16) * 8 + pair % 8 + 0.5
    quarter = np.where(pair % 16 < 8, 0.0, 0.25)
    origin = HALO_STEPS * LINES

    def wave(position):
        return np.cos(2 * np.pi * (np.outer(freq, position) / FREQS + quarter[:, None]))

    used = times[SPAN:].copy()
    valid = np.ones(used.shape, bool)
    valid[HALO_STEPS : HALO_STEPS + SPAN] = False
    valid &= used >= -(taps - 1 + SPAN)
    forward = wave((used + origin).reshape(-1)) * valid.reshape(1, -1)
    taps_wave = wave(np.arange(taps))
    halo_rows = times[SPAN + HALO_STEPS - SPAN : SPAN + HALO_STEPS].reshape(-1)
    main_rows = times[SPAN + HALO_STEPS + SPAN :].reshape(-1)
    back = wave(np.concatenate([halo_rows, main_rows]) + origin).T * (2.0 / FREQS)
    order = np.zeros((STEPS * LINES, STEPS * LINES), np.float32)
    order[main_rows, np.arange(main_rows.size)] = 1.0
    half = lambda a: np.asarray(a, np.float32).astype(ml_dtypes.bfloat16)
    return dict(
        forward=half(forward),
        taps_wave=split_wave(taps_wave),
        back=half(back),
        order=half(order),
    )


def split_wave(wave):
    high = np.asarray(wave, np.float32).astype(ml_dtypes.bfloat16)
    low = (wave - high.astype(np.float64)).astype(ml_dtypes.bfloat16)
    return np.concatenate([high, low, high], 1)


def lanes_of(group):
    return slice(group * LANES, (group + 1) * LANES)


def halves(values):
    high = values.astype(BF16)
    return high, (values - high.astype(F32)).astype(BF16)


def square_sums(table_ref, sums_ref):
    table = table_ref[...].astype(F32)
    high, low = halves(table * table)
    ones = jnp.ones((8, table.shape[1]), BF16)
    total = lax.dot_general(ones, high, NT, preferred_element_type=F32)
    total += lax.dot_general(ones, low, NT, preferred_element_type=F32)
    sums_ref[...] = jnp.broadcast_to(total[None, :1], sums_ref.shape)


def spectrum_of(wave_ref, medium_ref, spectrum_ref):
    high, low = halves(medium_ref[...])
    spectrum_ref[...] = jnp.dot(
        wave_ref[...], jnp.concatenate([high, high, low], 0), preferred_element_type=F32
    )


def one_hot(place, before, own, vocab):
    def digits(ids):
        high = lax.shift_right_arithmetic(ids, 4)
        low = ids - high * 16
        row = lax.broadcasted_iota(jnp.int32, (8, ids.shape[1]), 0)
        return jnp.where(row == 0, high, jnp.where(row == 1, low, 0)).astype(F32).astype(BF16)

    def picked(ids, first, steps, spread, shift):
        rows = steps * LINES
        row = lax.broadcasted_iota(jnp.int32, (rows, 1), 0)
        step = lax.shift_right_logical(row, 3)
        time = lax.bitwise_and(row, LINES - 1) * spread + step + shift
        column = lax.broadcasted_iota(jnp.int32, (rows, ids.shape[1]), 1) + first
        pick = jnp.where(column == time, 1.0, 0.0).astype(BF16)
        return lax.dot_general(pick, digits(ids), NT, preferred_element_type=F32)

    before = jnp.where(place > 0, before, -1)
    halo = picked(before, -HALO_IDS, SPAN + HALO_STEPS, HALO_STEPS, -LINES * HALO_STEPS - SPAN)
    edge = picked(before, -HALO_IDS, SPAN, STEPS, -SPAN)
    main = picked(own, 0, SPAN + STEPS, STEPS, -SPAN)
    column = jnp.concatenate([halo, edge + main[: SPAN * LINES], main[SPAN * LINES :]], 0)
    ids = (column[:, 0:1] * 16.0 + column[:, 1:2]).astype(jnp.int32)
    hot = ids == lax.broadcasted_iota(jnp.int32, (column.shape[0], vocab), 1)
    return jnp.where(hot, 1.0, 0.0).astype(BF16)


def taps_of(filters_ref, block, stream, group):
    return [
        jnp.broadcast_to(filters_ref[block, stream, d : d + 1, lanes_of(group)], (LINES, LANES))
        for d in range(SPAN + 1)
    ]


def tapped(window, taps, rows):
    total = None
    for d, tap in enumerate(taps):
        term = window[SPAN - d : SPAN - d + rows] * tap[None]
        total = term if total is None else total + term
    return total


def rows_at(start, size):
    return pl.ds(start if isinstance(start, int) else pl.multiple_of(start, 16), size)


def second_window(second_ref, b, group):
    rows = rows_at(b * BLOCK * LINES, (BLOCK + SPAN) * LINES)
    return second_ref[rows, lanes_of(group)].astype(F32).reshape(BLOCK + SPAN, LINES, LANES)


def driven_steps(driven_ref, b, group):
    rows = rows_at(b * BLOCK * LINES, BLOCK * LINES)
    return driven_ref[rows, lanes_of(group)].astype(F32).reshape(BLOCK, LINES, LANES)


def parts_of(kept_ref, modes):
    return (
        kept_ref.at[pl.ds(0, SECOND_ROWS)],
        kept_ref.at[pl.ds(SECOND_ROWS, STEPS * LINES)],
        kept_ref.at[pl.ds(SECOND_ROWS + STEPS * LINES, 2 * modes * LINES)],
    )


class Stage:
    def __init__(self, width, modes, kept_ref, ext_ref, gated_ref, query_ref, mixed_ref):
        self.width, self.modes = width, modes
        self.count = width // LANES
        self.second, self.driven, self.endings = parts_of(kept_ref, modes)
        self.ext, self.gated, self.query, self.mixed = ext_ref, gated_ref, query_ref, mixed_ref

    def embed(self, hot, scaled):
        rows = jnp.dot(hot, scaled, preferred_element_type=F32)
        self.ext[...] = rows.reshape(EXT_STEPS, LINES, self.width)

    def gate(self, filters_ref, at, steps):
        for g in range(self.count):
            window = self.ext[pl.ds(at, steps + SPAN), :, lanes_of(g)]
            key, value = [
                tapped(window, taps_of(filters_ref, 0, s, g), steps)
                for s in (1, 2)
            ]
            self.gated[rows_at(at * LINES, steps * LINES), lanes_of(g)] = (
                (key * value).reshape(steps * LINES, LANES).astype(BF16)
            )

    def ask(self, filters_ref, at, steps):
        for g in range(self.count):
            window = self.ext[pl.ds(at, steps + SPAN), :, lanes_of(g)]
            taps = taps_of(filters_ref, 0, 0, g)
            self.query[pl.ds(at, steps), :, lanes_of(g)] = tapped(window, taps, steps)

    def edges(self, filters_ref):
        gap = slice(HALO_STEPS * LINES, (HALO_STEPS + SPAN) * LINES)
        self.gated[gap, :] = jnp.zeros((SPAN * LINES, self.width), BF16)
        self.gate(filters_ref, 0, HALO_STEPS)
        self.ask(filters_ref, HALO_STEPS - SPAN, SPAN)

    def forward(self, forward_ref, spectrum_ref):
        wave = jnp.dot(forward_ref[...], self.gated[...], preferred_element_type=F32)
        wave = wave.reshape(FREQS // 16, 16, self.width)
        shape = spectrum_ref[...].reshape(FREQS // 16, 16, self.width)
        real, imag = wave[:, :8], wave[:, 8:]
        real_h, imag_h = shape[:, :8], shape[:, 8:]
        product = jnp.concatenate(
            [real * real_h - imag * imag_h, real * imag_h + imag * real_h], axis=1
        )
        self.mixed[...] = product.reshape(FREQS, self.width).astype(BF16)

    def backward(self, back_ref):
        middle = jnp.dot(back_ref[...], self.mixed[...], preferred_element_type=F32)
        middle = middle.reshape(SPAN + STEPS, LINES, self.width)
        halo = middle[:SPAN] * self.query[HALO_STEPS - SPAN : HALO_STEPS]
        halo = halo.astype(BF16).astype(F32)
        main = middle[SPAN:] * self.query[HALO_STEPS + SPAN :]
        main = main.reshape(STEPS * LINES, self.width).astype(BF16)
        self.second[SPAN * LINES :, :] = main
        last = main[(STEPS - SPAN) * LINES :].astype(F32).reshape(SPAN, LINES, self.width)
        first = []
        for k in range(SPAN):
            own = pltpu.roll(last[k], 1, 0)
            other = pltpu.roll(halo[k], 1, 0)
            line = lax.broadcasted_iota(jnp.int32, own.shape, 0)
            first.append(jnp.where(line == 0, other, own))
        self.second[: SPAN * LINES, :] = jnp.concatenate(first, 0).astype(BF16)

    def drive(self, filters_ref, b):
        for g in range(self.count):
            window = second_window(self.second, b, g)
            key, value = [
                tapped(window, taps_of(filters_ref, 1, s, g), BLOCK)
                for s in (1, 2)
            ]
            self.driven[rows_at(b * BLOCK * LINES, BLOCK * LINES), lanes_of(g)] = (
                (key * value).reshape(BLOCK * LINES, LANES).astype(BF16)
            )

    def decays(self, rates_ref, g):
        lanes = lanes_of(g)
        return [
            jnp.exp(-jnp.broadcast_to(rates_ref[r : r + 1, lanes], (LINES, LANES)))
            for r in range(self.modes)
        ]

    def absorb(self, decays, states, b, g):
        values = driven_steps(self.driven, b, g)
        for k in range(BLOCK):
            states = tuple(d * s + values[k] for d, s in zip(decays, states))
        return states

    def settle(self, rates_ref, state_ref, states, g):
        lanes = lanes_of(g)
        line = lax.broadcasted_iota(jnp.int32, (LINES, LANES), 0).astype(F32)
        for r in range(self.modes):
            self.endings[r * 2 * LINES : (r + 1) * 2 * LINES, lanes_of(g)] = jnp.concatenate(
                [h.astype(F32) for h in halves(states[r])], 0
            ).astype(BF16)
            weight = jnp.exp(-rates_ref[r : r + 1, lanes] * ((LINES - 1.0 - line) * STEPS))
            ending = jnp.sum(states[r] * weight, axis=0, keepdims=True).astype(state_ref.dtype)
            state_ref[0, r : r + 1, lanes] = ending


def first_part(
    channels,
    place_ref,
    squares_ref,
    before_ref,
    ids_ref,
    table_ref,
    gain_ref,
    filters_ref,
    rates_ref,
    forward_ref,
    spectrum_ref,
    back_ref,
    state_ref,
    kept_ref,
    ext_ref,
    gated_ref,
    query_ref,
    mixed_ref,
    forward_v,
    back_v,
    sems,
):
    loads = [
        pltpu.make_async_copy(forward_ref, forward_v, sems.at[0]),
        pltpu.make_async_copy(back_ref, back_v, sems.at[1]),
    ]
    for load in loads:
        load.start()
    vocab, width = table_ref.shape
    modes = rates_ref.shape[0]
    stage = Stage(width, modes, kept_ref, ext_ref, gated_ref, query_ref, mixed_ref)
    before = before_ref[:, before_ref.shape[1] - HALO_IDS :]
    hot = one_hot(place_ref[0], before, ids_ref[...], vocab)
    inverse = lax.rsqrt(jnp.sum(squares_ref[...], axis=0) / channels + 1e-06)
    column = jnp.transpose(jnp.broadcast_to(inverse, (8, vocab)))[:, 0:1]
    scaled = (table_ref[...].astype(F32) * column * gain_ref[...]).astype(BF16)
    main = HALO_STEPS + SPAN

    def loop(body):
        def step(i, carry):
            body(i)
            return carry

        lax.fori_loop(0, STEPS // BLOCK, step, 0)

    stage.embed(hot, scaled)
    stage.edges(filters_ref)

    def convolve(i):
        stage.gate(filters_ref, main + i * BLOCK, BLOCK)
        stage.ask(filters_ref, main + i * BLOCK, BLOCK)

    loop(convolve)
    loads[0].wait()
    stage.forward(forward_v, spectrum_ref)
    loads[1].wait()
    stage.backward(back_v)
    loop(lambda i: stage.drive(filters_ref, i))
    zero = jnp.zeros((LINES, LANES), F32)
    for g in range(stage.count):
        decays = stage.decays(rates_ref, g)

        def gather(i, states, g=g, decays=decays):
            return stage.absorb(decays, states, i, g)

        states = lax.fori_loop(0, STEPS // BLOCK, gather, (zero,) * modes)
        stage.settle(rates_ref, state_ref, states, g)
    for k in range(1, state_ref.shape[0]):
        state_ref[k] = state_ref[0]


def coefficients(rates, residues):
    double = 2.0 * rates
    series = double * (1.0 + double * (-0.5 + double * (1.0 / 6 + double * (-1.0 / 24))))
    return residues * jnp.sqrt(jnp.where(double < 0.02, series, 1.0 - jnp.exp(-double)))


def near_order(inner):
    late = inner // 2
    order = [late]
    for step in range(late):
        order += [place for place in (step, inner - step) if place % inner not in order and place < inner]
    order += [place for place in range(inner) if place not in order]
    return order[:0:-1] + order[:1]


def far_order(outer):
    return list(range(outer - 2, -1, -1)) + [outer - 1]


def near_part(place_ref, rows_ref, rates_ref, near_ref, total_ref):
    across = jnp.exp(-rates_ref[...] * (1.0 * STEPS * LINES))
    own = lax.rem(place_ref[0], rows_ref.shape[0])
    total = jnp.zeros(rates_ref.shape, F32)
    near = total
    order = near_order(rows_ref.shape[0])
    for j in range(rows_ref.shape[0]):
        near = jnp.where(own == j, total, near)
        total = across * total + rows_ref[order.index(j)].astype(F32)
    near_ref[...] = near
    total_ref[...] = jnp.broadcast_to(total.astype(BF16)[None], total_ref.shape)


def second_part(
    filters_ref,
    rates_ref,
    residues_ref,
    kept_ref,
    order_ref,
    query_ref,
    whole_ref,
    weights_ref,
    query_v,
    whole_v,
    order_v,
    sems,
):
    load = pltpu.make_async_copy(order_ref, order_v, sems.at[0])
    load.start()
    weights_ref[...] = coefficients(rates_ref[...], residues_ref[...])
    modes, width = rates_ref.shape
    groups = width // LANES
    index = lax.broadcasted_iota(jnp.int32, (LINES, LANES), 0)
    second_ref, driven_ref, endings_ref = parts_of(kept_ref, modes)
    for group in range(groups):
        taps = taps_of(filters_ref, 1, 0, group)

        def conv_query(b, carry, group=group, taps=taps):
            window = second_window(second_ref, b, group)
            rows = pl.ds(pl.multiple_of(b * BLOCK * LINES, BLOCK * LINES), BLOCK * LINES)
            query_v[rows, lanes_of(group)] = (
                tapped(window, taps, BLOCK).reshape(BLOCK * LINES, LANES).astype(BF16)
            )
            return carry

        lax.fori_loop(0, STEPS // BLOCK, conv_query, 0)

        decays, weights, starts = [], [], []
        for r in range(modes):
            rate = jnp.broadcast_to(rates_ref[r : r + 1, lanes_of(group)], (LINES, LANES))
            ending = endings_ref[r * 2 * LINES : (r + 1) * 2 * LINES, lanes_of(group)].astype(F32)
            total = ending[:LINES] + ending[LINES:]
            for k in (1, 2, 4):
                moved = jnp.where(index >= k, pltpu.roll(total, k, 0), 0.0)
                total = total + jnp.exp(-rate * (1.0 * STEPS * k)) * moved
            starts.append(jnp.where(index >= 1, pltpu.roll(total, 1, 0), 0.0))
            decays.append(jnp.exp(-rate))
            weights.append(
                jnp.broadcast_to(weights_ref[r : r + 1, lanes_of(group)], (LINES, LANES))
            )

        def respond(b, states, group=group, decays=decays, weights=weights):
            values = driven_steps(driven_ref, b, group)
            outs = []
            for k in range(BLOCK):
                states = tuple(d * s + values[k] for d, s in zip(decays, states))
                sums = [w * s for w, s in zip(weights, states)]
                while len(sums) > 1:
                    sums = [a + b for a, b in zip(sums[0::2], sums[1::2])]
                outs.append(sums[0])
            rows = pl.ds(pl.multiple_of(b * BLOCK * LINES, BLOCK * LINES), BLOCK * LINES)
            whole_v[rows, lanes_of(group)] = jnp.concatenate(outs, 0)
            return states

        lax.fori_loop(0, STEPS // BLOCK, respond, tuple(starts))
    load.wait()
    query_ref[...] = jnp.dot(
        order_v[...], query_v[...], preferred_element_type=F32
    ).astype(BF16)
    high, low = halves(whole_v[...])
    whole_ref[...] = jnp.dot(order_v[...], high, preferred_element_type=F32) + jnp.dot(
        order_v[...], low, preferred_element_type=F32
    )


def third_part(
    inner,
    place_ref,
    near_ref,
    totals_ref,
    rates_ref,
    weights_ref,
    query_ref,
    whole_ref,
    out_ref,
    result_v,
    sems,
):
    modes, width = rates_ref.shape
    groups = width // LANES
    span = 1.0 * STEPS * LINES
    across = jnp.exp(-rates_ref[...] * (span * inner))
    own = lax.rem(place_ref[0], inner)
    rank = lax.div(place_ref[0], inner)
    far = jnp.zeros(rates_ref.shape, F32)
    order = far_order(totals_ref.shape[0])
    for j in range(totals_ref.shape[0]):
        far = jnp.where(j < rank, across * far + totals_ref[order.index(j)].astype(F32), far)
    incoming = near_ref[...] + jnp.exp(-rates_ref[...] * (span * own.astype(F32))) * far

    stores = []
    across = jnp.exp(-rates_ref[...] * LINES)
    entering = weights_ref[...] * incoming
    line = lax.broadcasted_iota(jnp.int32, (LINES, LANES), 0).astype(F32)
    for group in range(groups):
        decays, terms = [], []
        for r in range(modes):
            decays.append(jnp.broadcast_to(across[r : r + 1, lanes_of(group)], (LINES, LANES)))
            rise = jnp.exp(-rates_ref[r : r + 1, lanes_of(group)] * (line + 1.0))
            terms.append(rise * entering[r : r + 1, lanes_of(group)])

        def lift(b, terms, group=group, decays=decays):
            rows = pl.ds(pl.multiple_of(b * 64, 64), 64)
            outs = []
            for k in range(8):
                sums = list(terms)
                while len(sums) > 1:
                    sums = [a + b for a, b in zip(sums[0::2], sums[1::2])]
                outs.append(sums[0])
                terms = tuple(t * d for t, d in zip(terms, decays))
            whole = whole_ref[rows, lanes_of(group)] + jnp.concatenate(outs, 0)
            query = query_ref[rows, lanes_of(group)].astype(F32)
            result_v[rows, lanes_of(group)] = (query * whole).astype(BF16)
            return terms

        lax.fori_loop(0, STEPS // 8, lift, tuple(terms))
        stores.append(
            pltpu.make_async_copy(
                result_v.at[:, lanes_of(group)], out_ref.at[:, lanes_of(group)], sems.at[group]
            )
        )
        stores[-1].start()
    for store in stores:
        store.wait()


VMEM = pl.BlockSpec(memory_space=pltpu.VMEM)
SMEM = pl.BlockSpec(memory_space=pltpu.SMEM)
HBM = pl.BlockSpec(memory_space=pl.ANY)


FAR = pl.BlockSpec(memory_space=pltpu.HBM)


def far(array):
    return pltpu.with_memory_space_constraint(jnp.asarray(array), pltpu.HBM)


def cost(flops, moved):
    return pl.CostEstimate(flops=int(flops), bytes_accessed=int(moved), transcendentals=0)


def call(
    kernel, name, ins, outs, scratch=(), sems=0, out_space=None, limit=24, flops=1e9, moved=4e6
):
    return pl.pallas_call(
        kernel,
        name=name,
        in_specs=ins,
        out_specs=[out_space or VMEM] * len(outs),
        out_shape=[jax.ShapeDtypeStruct(*o) for o in outs],
        scratch_shapes=[pltpu.VMEM(*s) for s in scratch]
        + ([pltpu.SemaphoreType.DMA((sems,))] if sems else []),
        compiler_params=pltpu.CompilerParams(vmem_limit_bytes=limit << 20),
        cost_estimate=cost(flops, moved),
    )


def local(
    token_ids, embed_table, norm_gain, short_filters, medium_filter, mode_rates, mode_residues
):
    vocab, width = embed_table.shape
    count = token_ids.shape[0]
    modes = mode_rates.shape[0]
    taps = medium_filter.shape[0]
    shards = lax.axis_size("ch")
    length = lax.axis_size("seq")
    inner = min(INNER, length)
    near_groups = [[o * inner + i for i in near_order(inner)] for o in range(length // inner)]
    far_groups = [[o * inner + i for o in far_order(length // inner)] for i in range(inner)]
    const = tables(taps)
    place = jnp.reshape(lax.axis_index("seq").astype(jnp.int32), (1,))

    before = lax.ppermute(token_ids, "seq", [(i, i + 1) for i in range(length - 1)])
    (partial,) = call(
        square_sums, "square_sums", [VMEM], [((shards, 1, vocab), F32)], limit=8
    )(embed_table)
    squares = lax.all_to_all(partial, "ch", 0, 0)
    (spectrum,) = call(
        spectrum_of, "spectrum_of", [VMEM] * 2, [((FREQS, width), F32)], limit=8
    )(const["taps_wave"], medium_filter)
    kept_shape = (SECOND_ROWS + STEPS * LINES + 2 * modes * LINES, width)
    state, kept = call(
        functools.partial(first_part, channels_of(width, shards)),
        "first_part",
        [SMEM] + [VMEM] * 7 + [FAR, VMEM, FAR],
        [((inner, modes, width), BF16), (kept_shape, BF16)],
        [
            ((EXT_STEPS, LINES, width), F32),
            ((OUT_STEPS * LINES, width), BF16),
            ((OUT_STEPS, LINES, width), F32),
            ((FREQS, width), BF16),
            (const["forward"].shape, BF16),
            (const["back"].shape, BF16),
        ],
        sems=2,
    )(
        place,
        squares,
        before[None],
        token_ids[None],
        embed_table,
        norm_gain[None],
        short_filters,
        mode_rates,
        far(const["forward"]),
        spectrum,
        far(const["back"]),
    )
    rows = lax.all_to_all(state, "seq", 0, 0, axis_index_groups=near_groups, tiled=True)
    query, whole, weights = call(
        second_part,
        "second_part",
        [VMEM] * 4 + [FAR],
        [((count, width), BF16), ((count, width), F32), ((modes, width), F32)],
        [((count, width), BF16), ((count, width), F32), ((count, count), BF16)],
        sems=1,
        flops=4e9,
        moved=1e7,
    )(short_filters, mode_rates, mode_residues, kept, far(const["order"]))
    near, totals = call(
        near_part,
        "near_part",
        [SMEM] + [VMEM] * 2,
        [((modes, width), F32), ((length // inner, modes, width), BF16)],
        limit=4,
    )(place, rows, mode_rates)
    totals = lax.all_to_all(totals, "seq", 0, 0, axis_index_groups=far_groups, tiled=True)
    (out,) = call(
        functools.partial(third_part, inner),
        "third_part",
        [SMEM] + [VMEM] * 6,
        [((count, width), BF16)],
        [((count, width), BF16)],
        sems=width // LANES,
        out_space=HBM,
        limit=12,
    )(place, near, totals, mode_rates, weights, query, whole)
    return out


def channels_of(width, shards):
    return width * shards


def solution(mesh):
    placed = (
        P("seq"),
        P(None, "ch"),
        P("ch"),
        P(None, None, None, "ch"),
        P(None, "ch"),
        P(None, "ch"),
        P(None, "ch"),
    )
    return jax.shard_map(
        local, mesh=mesh, in_specs=placed, out_specs=P("seq", "ch"), check_vma=False
    )
```

```python
import functools

import jax
import jax.numpy as jnp
import ml_dtypes
import numpy as np
from jax import lax
from jax.experimental import pallas as pl
from jax.experimental.pallas import tpu as pltpu
from jax.sharding import PartitionSpec as P

F32 = jnp.float32
BF16 = jnp.bfloat16
LANES = 128
STEPS = 64
LINES = 8
HALO_STEPS = 18
SPAN = 6
EXT_STEPS = SPAN + HALO_STEPS + SPAN + STEPS
OUT_STEPS = EXT_STEPS - SPAN
HALO_IDS = 256
BLOCK = 32
SECOND_ROWS = (SPAN + STEPS) * LINES
FREQS = 656
INNER = 8
NT = (((1,), (1,)), ((), ()))


def step_times():
    lines = np.arange(LINES)
    halo = -HALO_STEPS * LINES + lines[None] * HALO_STEPS + np.arange(-SPAN, HALO_STEPS)[:, None]
    main = lines[None] * STEPS + np.arange(-SPAN, STEPS)[:, None]
    return np.concatenate([halo, main], 0)


def tables(taps):
    times = step_times()
    pair = np.arange(FREQS)
    freq = (pair // 16) * 8 + pair % 8 + 0.5
    quarter = np.where(pair % 16 < 8, 0.0, 0.25)
    origin = HALO_STEPS * LINES

    def wave(position):
        return np.cos(2 * np.pi * (np.outer(freq, position) / FREQS + quarter[:, None]))

    used = times[SPAN:].copy()
    valid = np.ones(used.shape, bool)
    valid[HALO_STEPS : HALO_STEPS + SPAN] = False
    valid &= used >= -(taps - 1 + SPAN)
    forward = wave((used + origin).reshape(-1)) * valid.reshape(1, -1)
    taps_wave = wave(np.arange(taps))
    halo_rows = times[SPAN + HALO_STEPS - SPAN : SPAN + HALO_STEPS].reshape(-1)
    main_rows = times[SPAN + HALO_STEPS + SPAN :].reshape(-1)
    back = wave(np.concatenate([halo_rows, main_rows]) + origin).T * (2.0 / FREQS)
    order = np.zeros((STEPS * LINES, STEPS * LINES), np.float32)
    order[main_rows, np.arange(main_rows.size)] = 1.0
    half = lambda a: np.asarray(a, np.float32).astype(ml_dtypes.bfloat16)
    return dict(
        forward=half(forward),
        taps_wave=split_wave(taps_wave),
        back=half(back),
        order=half(order),
    )


def split_wave(wave):
    high = np.asarray(wave, np.float32).astype(ml_dtypes.bfloat16)
    low = (wave - high.astype(np.float64)).astype(ml_dtypes.bfloat16)
    return np.concatenate([high, low, high], 1)


def lanes_of(group):
    return slice(group * LANES, (group + 1) * LANES)


def halves(values):
    high = values.astype(BF16)
    return high, (values - high.astype(F32)).astype(BF16)


def square_sums(table_ref, sums_ref):
    table = table_ref[...].astype(F32)
    high, low = halves(table * table)
    ones = jnp.ones((8, table.shape[1]), BF16)
    total = lax.dot_general(ones, high, NT, preferred_element_type=F32)
    total += lax.dot_general(ones, low, NT, preferred_element_type=F32)
    sums_ref[...] = jnp.broadcast_to(total[None, :1], sums_ref.shape)


def spectrum_of(wave_ref, medium_ref, spectrum_ref):
    high, low = halves(medium_ref[...])
    spectrum_ref[...] = jnp.dot(
        wave_ref[...], jnp.concatenate([high, high, low], 0), preferred_element_type=F32
    )


def one_hot(place, before, own, vocab):
    def digits(ids):
        high = lax.shift_right_arithmetic(ids, 4)
        low = ids - high * 16
        row = lax.broadcasted_iota(jnp.int32, (8, ids.shape[1]), 0)
        return jnp.where(row == 0, high, jnp.where(row == 1, low, 0)).astype(F32).astype(BF16)

    def picked(ids, first, steps, spread, shift):
        rows = steps * LINES
        row = lax.broadcasted_iota(jnp.int32, (rows, 1), 0)
        step = lax.shift_right_logical(row, 3)
        time = lax.bitwise_and(row, LINES - 1) * spread + step + shift
        column = lax.broadcasted_iota(jnp.int32, (rows, ids.shape[1]), 1) + first
        pick = jnp.where(column == time, 1.0, 0.0).astype(BF16)
        return lax.dot_general(pick, digits(ids), NT, preferred_element_type=F32)

    before = jnp.where(place > 0, before, -1)
    halo = picked(before, -HALO_IDS, SPAN + HALO_STEPS, HALO_STEPS, -LINES * HALO_STEPS - SPAN)
    edge = picked(before, -HALO_IDS, SPAN, STEPS, -SPAN)
    main = picked(own, 0, SPAN + STEPS, STEPS, -SPAN)
    column = jnp.concatenate([halo, edge + main[: SPAN * LINES], main[SPAN * LINES :]], 0)
    ids = (column[:, 0:1] * 16.0 + column[:, 1:2]).astype(jnp.int32)
    hot = ids == lax.broadcasted_iota(jnp.int32, (column.shape[0], vocab), 1)
    return jnp.where(hot, 1.0, 0.0).astype(BF16)


def taps_of(filters_ref, block, stream, group):
    return [
        jnp.broadcast_to(filters_ref[block, stream, d : d + 1, lanes_of(group)], (LINES, LANES))
        for d in range(SPAN + 1)
    ]


def tapped(window, taps, rows):
    total = None
    for d, tap in enumerate(taps):
        term = window[SPAN - d : SPAN - d + rows] * tap[None]
        total = term if total is None else total + term
    return total


def rows_at(start, size):
    return pl.ds(start if isinstance(start, int) else pl.multiple_of(start, 16), size)


def second_window(second_ref, b, group):
    rows = rows_at(b * BLOCK * LINES, (BLOCK + SPAN) * LINES)
    return second_ref[rows, lanes_of(group)].astype(F32).reshape(BLOCK + SPAN, LINES, LANES)


def driven_steps(driven_ref, b, group):
    rows = rows_at(b * BLOCK * LINES, BLOCK * LINES)
    return driven_ref[rows, lanes_of(group)].astype(F32).reshape(BLOCK, LINES, LANES)


def parts_of(kept_ref, modes):
    return (
        kept_ref.at[pl.ds(0, SECOND_ROWS)],
        kept_ref.at[pl.ds(SECOND_ROWS, STEPS * LINES)],
        kept_ref.at[pl.ds(SECOND_ROWS + STEPS * LINES, 2 * modes * LINES)],
    )


class Stage:
    def __init__(self, width, modes, kept_ref, ext_ref, gated_ref, query_ref, mixed_ref):
        self.width, self.modes = width, modes
        self.count = width // LANES
        self.second, self.driven, self.endings = parts_of(kept_ref, modes)
        self.ext, self.gated, self.query, self.mixed = ext_ref, gated_ref, query_ref, mixed_ref

    def embed(self, hot, scaled):
        rows = jnp.dot(hot, scaled, preferred_element_type=F32)
        self.ext[...] = rows.reshape(EXT_STEPS, LINES, self.width)

    def gate(self, filters_ref, at, steps):
        for g in range(self.count):
            window = self.ext[pl.ds(at, steps + SPAN), :, lanes_of(g)]
            key, value = [
                tapped(window, taps_of(filters_ref, 0, s, g), steps)
                for s in (1, 2)
            ]
            self.gated[rows_at(at * LINES, steps * LINES), lanes_of(g)] = (
                (key * value).reshape(steps * LINES, LANES).astype(BF16)
            )

    def ask(self, filters_ref, at, steps):
        for g in range(self.count):
            window = self.ext[pl.ds(at, steps + SPAN), :, lanes_of(g)]
            taps = taps_of(filters_ref, 0, 0, g)
            self.query[pl.ds(at, steps), :, lanes_of(g)] = tapped(window, taps, steps)

    def edges(self, filters_ref):
        gap = slice(HALO_STEPS * LINES, (HALO_STEPS + SPAN) * LINES)
        self.gated[gap, :] = jnp.zeros((SPAN * LINES, self.width), BF16)
        self.gate(filters_ref, 0, HALO_STEPS)
        self.ask(filters_ref, HALO_STEPS - SPAN, SPAN)

    def forward(self, forward_ref, spectrum_ref):
        wave = jnp.dot(forward_ref[...], self.gated[...], preferred_element_type=F32)
        wave = wave.reshape(FREQS // 16, 16, self.width)
        shape = spectrum_ref[...].reshape(FREQS // 16, 16, self.width)
        real, imag = wave[:, :8], wave[:, 8:]
        real_h, imag_h = shape[:, :8], shape[:, 8:]
        product = jnp.concatenate(
            [real * real_h - imag * imag_h, real * imag_h + imag * real_h], axis=1
        )
        self.mixed[...] = product.reshape(FREQS, self.width).astype(BF16)

    def backward(self, back_ref):
        middle = jnp.dot(back_ref[...], self.mixed[...], preferred_element_type=F32)
        middle = middle.reshape(SPAN + STEPS, LINES, self.width)
        halo = middle[:SPAN] * self.query[HALO_STEPS - SPAN : HALO_STEPS]
        halo = halo.astype(BF16).astype(F32)
        main = middle[SPAN:] * self.query[HALO_STEPS + SPAN :]
        main = main.reshape(STEPS * LINES, self.width).astype(BF16)
        self.second[SPAN * LINES :, :] = main
        last = main[(STEPS - SPAN) * LINES :].astype(F32).reshape(SPAN, LINES, self.width)
        first = []
        for k in range(SPAN):
            own = pltpu.roll(last[k], 1, 0)
            other = pltpu.roll(halo[k], 1, 0)
            line = lax.broadcasted_iota(jnp.int32, own.shape, 0)
            first.append(jnp.where(line == 0, other, own))
        self.second[: SPAN * LINES, :] = jnp.concatenate(first, 0).astype(BF16)

    def drive(self, filters_ref, b):
        for g in range(self.count):
            window = second_window(self.second, b, g)
            key, value = [
                tapped(window, taps_of(filters_ref, 1, s, g), BLOCK)
                for s in (1, 2)
            ]
            self.driven[rows_at(b * BLOCK * LINES, BLOCK * LINES), lanes_of(g)] = (
                (key * value).reshape(BLOCK * LINES, LANES).astype(BF16)
            )

    def decays(self, rates_ref, g):
        lanes = lanes_of(g)
        return [
            jnp.exp(-jnp.broadcast_to(rates_ref[r : r + 1, lanes], (LINES, LANES)))
            for r in range(self.modes)
        ]

    def absorb(self, decays, states, b, g):
        values = driven_steps(self.driven, b, g)
        for k in range(BLOCK):
            states = tuple(d * s + values[k] for d, s in zip(decays, states))
        return states

    def settle(self, rates_ref, state_ref, states, g):
        lanes = lanes_of(g)
        line = lax.broadcasted_iota(jnp.int32, (LINES, LANES), 0).astype(F32)
        for r in range(self.modes):
            self.endings[r * 2 * LINES : (r + 1) * 2 * LINES, lanes_of(g)] = jnp.concatenate(
                [h.astype(F32) for h in halves(states[r])], 0
            ).astype(BF16)
            weight = jnp.exp(-rates_ref[r : r + 1, lanes] * ((LINES - 1.0 - line) * STEPS))
            ending = jnp.sum(states[r] * weight, axis=0, keepdims=True).astype(state_ref.dtype)
            state_ref[0, r : r + 1, lanes] = ending


def first_part(
    channels,
    place_ref,
    squares_ref,
    before_ref,
    ids_ref,
    table_ref,
    gain_ref,
    filters_ref,
    rates_ref,
    forward_ref,
    spectrum_ref,
    back_ref,
    state_ref,
    kept_ref,
    ext_ref,
    gated_ref,
    query_ref,
    mixed_ref,
    forward_v,
    back_v,
    sems,
):
    loads = [
        pltpu.make_async_copy(forward_ref, forward_v, sems.at[0]),
        pltpu.make_async_copy(back_ref, back_v, sems.at[1]),
    ]
    for load in loads:
        load.start()
    vocab, width = table_ref.shape
    modes = rates_ref.shape[0]
    stage = Stage(width, modes, kept_ref, ext_ref, gated_ref, query_ref, mixed_ref)
    before = before_ref[:, before_ref.shape[1] - HALO_IDS :]
    hot = one_hot(place_ref[0], before, ids_ref[...], vocab)
    inverse = lax.rsqrt(jnp.sum(squares_ref[...], axis=0) / channels + 1e-06)
    column = jnp.transpose(jnp.broadcast_to(inverse, (8, vocab)))[:, 0:1]
    scaled = (table_ref[...].astype(F32) * column * gain_ref[...]).astype(BF16)
    main = HALO_STEPS + SPAN

    def loop(body):
        def step(i, carry):
            body(i)
            return carry

        lax.fori_loop(0, STEPS // BLOCK, step, 0)

    stage.embed(hot, scaled)
    stage.edges(filters_ref)

    def convolve(i):
        stage.gate(filters_ref, main + i * BLOCK, BLOCK)
        stage.ask(filters_ref, main + i * BLOCK, BLOCK)

    loop(convolve)
    loads[0].wait()
    stage.forward(forward_v, spectrum_ref)
    loads[1].wait()
    stage.backward(back_v)
    loop(lambda i: stage.drive(filters_ref, i))
    zero = jnp.zeros((LINES, LANES), F32)
    for g in range(stage.count):
        decays = stage.decays(rates_ref, g)

        def gather(i, states, g=g, decays=decays):
            return stage.absorb(decays, states, i, g)

        states = lax.fori_loop(0, STEPS // BLOCK, gather, (zero,) * modes)
        stage.settle(rates_ref, state_ref, states, g)
    for k in range(1, state_ref.shape[0]):
        state_ref[k] = state_ref[0]


def coefficients(rates, residues):
    double = 2.0 * rates
    series = double * (1.0 + double * (-0.5 + double * (1.0 / 6 + double * (-1.0 / 24))))
    return residues * jnp.sqrt(jnp.where(double < 0.02, series, 1.0 - jnp.exp(-double)))


def near_order(inner):
    late = inner // 2
    order = [late]
    for step in range(late):
        order += [place for place in (step, inner - step) if place % inner not in order and place < inner]
    order += [place for place in range(inner) if place not in order]
    return order[:0:-1] + order[:1]


def far_order(outer):
    return list(range(outer - 2, -1, -1)) + [outer - 1]


def near_part(place_ref, rows_ref, rates_ref, near_ref, total_ref):
    across = jnp.exp(-rates_ref[...] * (1.0 * STEPS * LINES))
    own = lax.rem(place_ref[0], rows_ref.shape[0])
    total = jnp.zeros(rates_ref.shape, F32)
    near = total
    order = near_order(rows_ref.shape[0])
    for j in range(rows_ref.shape[0]):
        near = jnp.where(own == j, total, near)
        total = across * total + rows_ref[order.index(j)].astype(F32)
    near_ref[...] = near
    total_ref[...] = jnp.broadcast_to(total.astype(BF16)[None], total_ref.shape)


def second_part(
    filters_ref,
    rates_ref,
    residues_ref,
    kept_ref,
    order_ref,
    query_ref,
    whole_ref,
    weights_ref,
    query_v,
    whole_v,
    order_v,
    sems,
):
    load = pltpu.make_async_copy(order_ref, order_v, sems.at[0])
    load.start()
    weights_ref[...] = coefficients(rates_ref[...], residues_ref[...])
    modes, width = rates_ref.shape
    groups = width // LANES
    index = lax.broadcasted_iota(jnp.int32, (LINES, LANES), 0)
    second_ref, driven_ref, endings_ref = parts_of(kept_ref, modes)
    for group in range(groups):
        taps = taps_of(filters_ref, 1, 0, group)

        def conv_query(b, carry, group=group, taps=taps):
            window = second_window(second_ref, b, group)
            rows = pl.ds(pl.multiple_of(b * BLOCK * LINES, BLOCK * LINES), BLOCK * LINES)
            query_v[rows, lanes_of(group)] = (
                tapped(window, taps, BLOCK).reshape(BLOCK * LINES, LANES).astype(BF16)
            )
            return carry

        lax.fori_loop(0, STEPS // BLOCK, conv_query, 0)

        decays, weights, starts = [], [], []
        for r in range(modes):
            rate = jnp.broadcast_to(rates_ref[r : r + 1, lanes_of(group)], (LINES, LANES))
            ending = endings_ref[r * 2 * LINES : (r + 1) * 2 * LINES, lanes_of(group)].astype(F32)
            total = ending[:LINES] + ending[LINES:]
            for k in (1, 2, 4):
                moved = jnp.where(index >= k, pltpu.roll(total, k, 0), 0.0)
                total = total + jnp.exp(-rate * (1.0 * STEPS * k)) * moved
            starts.append(jnp.where(index >= 1, pltpu.roll(total, 1, 0), 0.0))
            decays.append(jnp.exp(-rate))
            weights.append(
                jnp.broadcast_to(weights_ref[r : r + 1, lanes_of(group)], (LINES, LANES))
            )

        def respond(b, states, group=group, decays=decays, weights=weights):
            values = driven_steps(driven_ref, b, group)
            outs = []
            for k in range(BLOCK):
                states = tuple(d * s + values[k] for d, s in zip(decays, states))
                sums = [w * s for w, s in zip(weights, states)]
                while len(sums) > 1:
                    sums = [a + b for a, b in zip(sums[0::2], sums[1::2])]
                outs.append(sums[0])
            rows = pl.ds(pl.multiple_of(b * BLOCK * LINES, BLOCK * LINES), BLOCK * LINES)
            whole_v[rows, lanes_of(group)] = jnp.concatenate(outs, 0)
            return states

        lax.fori_loop(0, STEPS // BLOCK, respond, tuple(starts))
    load.wait()
    query_ref[...] = jnp.dot(
        order_v[...], query_v[...], preferred_element_type=F32
    ).astype(BF16)
    high, low = halves(whole_v[...])
    whole_ref[...] = jnp.dot(order_v[...], high, preferred_element_type=F32) + jnp.dot(
        order_v[...], low, preferred_element_type=F32
    )


def third_part(
    inner,
    place_ref,
    near_ref,
    totals_ref,
    rates_ref,
    weights_ref,
    query_ref,
    whole_ref,
    out_ref,
    result_v,
    sems,
):
    modes, width = rates_ref.shape
    groups = width // LANES
    span = 1.0 * STEPS * LINES
    across = jnp.exp(-rates_ref[...] * (span * inner))
    own = lax.rem(place_ref[0], inner)
    rank = lax.div(place_ref[0], inner)
    far = jnp.zeros(rates_ref.shape, F32)
    order = far_order(totals_ref.shape[0])
    for j in range(totals_ref.shape[0]):
        far = jnp.where(j < rank, across * far + totals_ref[order.index(j)].astype(F32), far)
    incoming = near_ref[...] + jnp.exp(-rates_ref[...] * (span * own.astype(F32))) * far

    stores = []
    across = jnp.exp(-rates_ref[...] * LINES)
    entering = weights_ref[...] * incoming
    line = lax.broadcasted_iota(jnp.int32, (LINES, LANES), 0).astype(F32)
    for group in range(groups):
        decays, terms = [], []
        for r in range(modes):
            decays.append(jnp.broadcast_to(across[r : r + 1, lanes_of(group)], (LINES, LANES)))
            rise = jnp.exp(-rates_ref[r : r + 1, lanes_of(group)] * (line + 1.0))
            terms.append(rise * entering[r : r + 1, lanes_of(group)])

        def lift(b, terms, group=group, decays=decays):
            rows = pl.ds(pl.multiple_of(b * 64, 64), 64)
            outs = []
            for k in range(8):
                sums = list(terms)
                while len(sums) > 1:
                    sums = [a + b for a, b in zip(sums[0::2], sums[1::2])]
                outs.append(sums[0])
                terms = tuple(t * d for t, d in zip(terms, decays))
            whole = whole_ref[rows, lanes_of(group)] + jnp.concatenate(outs, 0)
            query = query_ref[rows, lanes_of(group)].astype(F32)
            result_v[rows, lanes_of(group)] = (query * whole).astype(BF16)
            return terms

        lax.fori_loop(0, STEPS // 8, lift, tuple(terms))
        stores.append(
            pltpu.make_async_copy(
                result_v.at[:, lanes_of(group)], out_ref.at[:, lanes_of(group)], sems.at[group]
            )
        )
        stores[-1].start()
    for store in stores:
        store.wait()


VMEM = pl.BlockSpec(memory_space=pltpu.VMEM)
SMEM = pl.BlockSpec(memory_space=pltpu.SMEM)
HBM = pl.BlockSpec(memory_space=pl.ANY)


FAR = pl.BlockSpec(memory_space=pltpu.HBM)


def far(array):
    return pltpu.with_memory_space_constraint(jnp.asarray(array), pltpu.HBM)


def cost(flops, moved):
    return pl.CostEstimate(flops=int(flops), bytes_accessed=int(moved), transcendentals=0)


def call(
    kernel, name, ins, outs, scratch=(), sems=0, out_space=None, limit=24, flops=1e9, moved=4e6
):
    return pl.pallas_call(
        kernel,
        name=name,
        in_specs=ins,
        out_specs=[out_space or VMEM] * len(outs),
        out_shape=[jax.ShapeDtypeStruct(*o) for o in outs],
        scratch_shapes=[pltpu.VMEM(*s) for s in scratch]
        + ([pltpu.SemaphoreType.DMA((sems,))] if sems else []),
        compiler_params=pltpu.CompilerParams(vmem_limit_bytes=limit << 20),
        cost_estimate=cost(flops, moved),
    )


def local(
    token_ids, embed_table, norm_gain, short_filters, medium_filter, mode_rates, mode_residues
):
    vocab, width = embed_table.shape
    count = token_ids.shape[0]
    modes = mode_rates.shape[0]
    taps = medium_filter.shape[0]
    shards = lax.axis_size("ch")
    length = lax.axis_size("seq")
    inner = min(INNER, length)
    near_groups = [[o * inner + i for i in near_order(inner)] for o in range(length // inner)]
    far_groups = [[o * inner + i for o in far_order(length // inner)] for i in range(inner)]
    const = tables(taps)
    place = jnp.reshape(lax.axis_index("seq").astype(jnp.int32), (1,))

    before = lax.ppermute(token_ids, "seq", [(i, i + 1) for i in range(length - 1)])
    (partial,) = call(
        square_sums, "square_sums", [VMEM], [((shards, 1, vocab), F32)], limit=8
    )(embed_table)
    squares = lax.all_to_all(partial, "ch", 0, 0)
    (spectrum,) = call(
        spectrum_of, "spectrum_of", [VMEM] * 2, [((FREQS, width), F32)], limit=8
    )(const["taps_wave"], medium_filter)
    kept_shape = (SECOND_ROWS + STEPS * LINES + 2 * modes * LINES, width)
    state, kept = call(
        functools.partial(first_part, channels_of(width, shards)),
        "first_part",
        [SMEM] + [VMEM] * 7 + [FAR, VMEM, FAR],
        [((inner, modes, width), BF16), (kept_shape, BF16)],
        [
            ((EXT_STEPS, LINES, width), F32),
            ((OUT_STEPS * LINES, width), BF16),
            ((OUT_STEPS, LINES, width), F32),
            ((FREQS, width), BF16),
            (const["forward"].shape, BF16),
            (const["back"].shape, BF16),
        ],
        sems=2,
    )(
        place,
        squares,
        before[None],
        token_ids[None],
        embed_table,
        norm_gain[None],
        short_filters,
        mode_rates,
        far(const["forward"]),
        spectrum,
        far(const["back"]),
    )
    rows = lax.all_to_all(state, "seq", 0, 0, axis_index_groups=near_groups, tiled=True)
    query, whole, weights = call(
        second_part,
        "second_part",
        [VMEM] * 4 + [FAR],
        [((count, width), BF16), ((count, width), F32), ((modes, width), F32)],
        [((count, width), BF16), ((count, width), F32), ((count, count), BF16)],
        sems=1,
        flops=4e9,
        moved=1e7,
    )(short_filters, mode_rates, mode_residues, kept, far(const["order"]))
    near, totals = call(
        near_part,
        "near_part",
        [SMEM] + [VMEM] * 2,
        [((modes, width), F32), ((length // inner, modes, width), BF16)],
        limit=4,
    )(place, rows, mode_rates)
    totals = lax.all_to_all(totals, "seq", 0, 0, axis_index_groups=far_groups, tiled=True)
    (out,) = call(
        functools.partial(third_part, inner),
        "third_part",
        [SMEM] + [VMEM] * 6,
        [((count, width), BF16)],
        [((count, width), BF16)],
        sems=width // LANES,
        out_space=HBM,
        limit=12,
    )(place, near, totals, mode_rates, weights, query, whole)
    return out


def channels_of(width, shards):
    return width * shards


def solution(mesh):
    placed = (
        P("seq"),
        P(None, "ch"),
        P("ch"),
        P(None, None, None, "ch"),
        P(None, "ch"),
        P(None, "ch"),
        P(None, "ch"),
    )
    return jax.shard_map(
        local, mesh=mesh, in_specs=placed, out_specs=P("seq", "ch"), check_vma=False
    )
```
